512 devices in a mesh: rep: 64 (over z, y), loop: 8 (over x, core).
Axes of the slice: x: 4, y: 4, z: 16, core: 2. Of those that a mesh axis runs over, the one named last changes fastest.
Arguments:
- features: bfloat16 [65536, 256], P(('rep', 'loop')), may hold values from -6 to 6
- tiles: bfloat16 [49152, 128, 128], P(('rep', 'loop'))
- tile_dst: int32 [49152], P(('rep', 'loop')), may hold values from 0 to 7
- tile_src: int32 [49152], P(('rep', 'loop')), may hold values from 0 to 63
- tile_count: int32 [512], P(('rep', 'loop')), may hold values from 24 to 96, as said below
- weights: bfloat16 [2, 256, 256], replicated, may hold values from -0.375 to 0.375
- biases: float32 [2, 256], replicated, may hold values from -3 to 3
Outputs:
- hidden_out: bfloat16 [65536, 256], P(('rep', 'loop'))
The draws below stay inside these ranges and needn't reach their ends.
Inputs may be any that keep to these rules, and one draw needn't show every extreme that they name: `tile_count`: some device in every draw has all 96 slots occupied.
All inputs are finite; a program needn't handle non-finite values.
Results may differ from the reference program's by a relative error of at most 0.019.
Values may be sent and summed in bfloat16 or wider, within the bound.
A program may use at most 64 MiB of HBM per device.

```python
import math
import jax
import jax.numpy as jnp
from jax import lax

F = 256
BLOCK = 128
TILES_DEV = 96
LAYERS = 2
NODES = 65536
SLOTS = 49152
N_REP = 64
N_LOOP = 8


def draw_tiles(key, part):
    key = jax.random.fold_in(key, 2)
    shape = (TILES_DEV * N_REP * N_LOOP, BLOCK, BLOCK)
    key_dense, key_mask, key_vals = jax.random.split(key, 3)
    density = jnp.exp(jax.random.uniform(key_dense, (shape[0], 1, 1), jnp.float32, math.log(0.03), math.log(0.6)))
    mask = (jax.random.uniform(key_mask, shape, jnp.float32) < density).astype(jnp.float32)
    scale = 1.0 / jnp.sqrt(BLOCK * density * TILES_DEV * 0.5)
    values = jax.random.normal(key_vals, shape, jnp.float32)
    return (values * mask * scale).astype(jnp.bfloat16)


def draw_tile_count(key, part):
    key = jax.random.fold_in(key, 1)
    key_div, key_full = jax.random.split(key)
    devices_all = N_REP * N_LOOP
    divisor = jax.random.randint(key_div, (devices_all,), 1, 5)
    counts = TILES_DEV // divisor
    fullest = jax.random.randint(key_full, (), 0, devices_all)
    return counts.at[fullest].set(TILES_DEV).astype(jnp.int32)


def touch_ends(drawn, stream_key, low, top_value):
    longest = drawn.shape.index(max(drawn.shape))
    spots = []
    for shift in (0, 1):
        where = [jax.random.randint(jax.random.fold_in(stream_key, axis), (), 0, length) for axis, length in enumerate(drawn.shape)]
        where[longest] = (where[longest] + shift) % drawn.shape[longest]
        spots.append(tuple(where))
    return drawn.at[spots[0]].set(low).at[spots[1]].set(top_value)


def steps_of(key, extent, pieces, least, largest):
    level = 1.0
    for axis_at, blocks in pieces:
        draws = jax.random.uniform(jax.random.fold_in(jax.random.fold_in(key, 6), axis_at), (blocks,), jnp.float32, least / len(pieces), largest / len(pieces))
        level = level * jnp.repeat(jnp.exp(draws), extent[axis_at] // blocks).reshape((-1,) + (1,) * (len(extent) - 1 - axis_at))
    return level


def normal_values(stream_key, extent, deviation, most, shards=(), held_as=jnp.bfloat16):
    result = deviation * jax.random.normal(stream_key, extent, jnp.float32)
    if shards:
        result = result * steps_of(stream_key, extent, shards, -0.22, 0.18)
    return jnp.clip(result, -most, most).astype(held_as)


def setup_inputs(seed: int = 0) -> dict:
    key_list = jax.random.split(jax.random.key(seed), 8)
    features = normal_values(key_list[0], (NODES, F), 1.0, 6.0, ((0, 512),))
    tiles = draw_tiles(jax.random.fold_in(key_list[7], 71), 0)
    tile_dst = touch_ends(jax.random.randint(key_list[2], (SLOTS,), 0, N_LOOP), jax.random.fold_in(key_list[2], 1), 0, N_LOOP - 1).astype(jnp.int32)
    tile_src = touch_ends(jax.random.randint(key_list[3], (SLOTS,), 0, N_REP), jax.random.fold_in(key_list[3], 1), 0, N_REP - 1).astype(jnp.int32)
    tile_count = draw_tile_count(jax.random.fold_in(key_list[7], 71), 0)
    weights = normal_values(key_list[5], (LAYERS, F, F), F ** -0.5, 0.375)
    biases = normal_values(key_list[6], (LAYERS, F), 0.5, 3.0, (), jnp.float32)
    return {"features": features, "tiles": tiles, "tile_dst": tile_dst, "tile_src": tile_src, "tile_count": tile_count, "weights": weights, "biases": biases}


def one_layer(hidden, tiles, tile_dst, tile_src, tile_count, weight, bias):
    devices_all = N_REP * N_LOOP
    blocks_all = hidden.reshape(devices_all, BLOCK, F)
    tiles_dev = tiles.reshape(devices_all, TILES_DEV, BLOCK, BLOCK)
    dst_dev = tile_dst.reshape(devices_all, TILES_DEV)
    src_dev = tile_src.reshape(devices_all, TILES_DEV)
    lanes = jnp.arange(N_LOOP, dtype=jnp.int32)
    slot_ids = jnp.arange(TILES_DEV, dtype=jnp.int32)

    def per_device(total, device):
        group = device // N_LOOP
        column = device % N_LOOP
        sources = blocks_all[src_dev[device] * N_LOOP + column]
        products = jnp.einsum('tab,tbf->taf', tiles_dev[device].astype(jnp.float32), sources.astype(jnp.float32))
        valid = slot_ids < tile_count[device]
        select = ((dst_dev[device][:, None] == lanes[None, :]) & valid[:, None]).astype(jnp.float32)
        contrib = jnp.einsum('tj,taf->jaf', select, products)
        start = (group * N_LOOP).astype(jnp.int32)
        old = lax.dynamic_slice_in_dim(total, start, N_LOOP, 0)
        total = lax.dynamic_update_slice_in_dim(total, old + contrib, start, 0)
        return total, None

    total, unused = lax.scan(per_device, jnp.zeros((devices_all, BLOCK, F), jnp.float32), jnp.arange(devices_all, dtype=jnp.int32))
    aggregate = total.reshape(devices_all * BLOCK, F).astype(jnp.bfloat16)
    mixed = jnp.dot(aggregate, weight, preferred_element_type=jnp.float32) + bias[None, :]
    return jax.nn.relu(mixed).astype(jnp.bfloat16)


def reference(features, tiles, tile_dst, tile_src, tile_count, weights, biases):
    hidden = features
    for layer in range(LAYERS):
        hidden = one_layer(hidden, tiles, tile_dst, tile_src, tile_count, weights[layer], biases[layer])
    return hidden
```

```python
import jax
import jax.numpy as jnp
from jax import lax
from jax.experimental import pallas as pl
from jax.experimental.pallas import tpu as pltpu
from jax.sharding import PartitionSpec as P

MESH = pl.DeviceIdType.MESH
NZ, NY, NL = 16, 4, 8
NREP = NZ * NY
B = 128
F = 256
SLOTS = 96
LAYERS = 2
CH = 2
FC = F // CH
RA = 48
RB = B - RA
PAIRS = (SLOTS + NL) // 2
PIECES_A = 2 * 8
NSEM = 96
LAG = 4


def order_tables(dst, src, count):
    n = SLOTS
    i32 = jnp.int32
    row = lax.broadcasted_iota(i32, (n, n), 0)
    col = lax.broadcasted_iota(i32, (n, n), 1)
    eye = row == col
    lane = lax.broadcasted_iota(i32, (1, n), 1)
    key_row = jnp.where(lane < count, dst, NL)
    key_col = jnp.sum(jnp.where(eye, key_row, 0), axis=1, keepdims=True)
    src_col = jnp.sum(jnp.where(eye, src, 0), axis=1, keepdims=True)
    rank = jnp.sum(jnp.where((key_col == key_row) & (col < row), 1, 0), axis=1, keepdims=True)
    lanes = lax.broadcasted_iota(i32, (n, B), 1)
    onehot = key_col == lanes
    number = jnp.sum(jnp.where(onehot, 1, 0), axis=0, keepdims=True)
    lane_b = lax.broadcasted_iota(i32, (1, B), 1)
    number = jnp.where(lane_b < NL, number, 0)
    pairs = (number + 1) // 2
    row_b = lax.broadcasted_iota(i32, (B, B), 0)
    col_b = lax.broadcasted_iota(i32, (B, B), 1)
    pairs_col = jnp.sum(jnp.where(row_b == col_b, pairs, 0), axis=1, keepdims=True)
    first = jnp.sum(jnp.where(row_b < col_b, pairs_col, 0), axis=0, keepdims=True)
    first_col = jnp.sum(jnp.where(row_b == col_b, first, 0), axis=1, keepdims=True)
    start = jnp.sum(jnp.where(onehot, first, 0), axis=1, keepdims=True)
    place = jnp.where(key_col < NL, 2 * start + rank, B)
    here = place == lanes
    slot_col = lax.broadcasted_iota(i32, (n, B), 0)
    slot = SLOTS + jnp.sum(jnp.where(here, slot_col - SLOTS, 0), axis=0, keepdims=True)
    source = jnp.sum(jnp.where(here, src_col, 0), axis=0, keepdims=True)
    opens = jnp.sum(jnp.where((first_col == col_b) & (pairs_col > 0), 1, 0), axis=0, keepdims=True)
    last = jnp.where(pairs > 0, first + pairs - 1, -1)
    return slot, source, 1 - opens, last


def kernel(
    features,
    tiles_hbm,
    dst_ref,
    src_ref,
    count_ref,
    weights,
    biases,
    out,
    h00,
    h01,
    h10,
    h11,
    tiles,
    table_v,
    table,
    runs0,
    runs1,
    outbox,
    inbox,
    own_sum,
    send_sems,
    recv_sems,
    local_sems,
):
    rep = lax.axis_index("rep")
    me = lax.axis_index("loop")
    z = rep // NY
    y = rep % NY
    held = ((h00, h01), (h10, h11))
    runs = (runs0, runs1)

    def zmod(v):
        return lax.rem(v + 2 * NZ, NZ)

    def ymod(v):
        return lax.rem(v + 2 * NY, NY)

    def at(zz, yy):
        return {"rep": zz * NY + yy}

    z_up, z_down = at(zmod(z + 1), y), at(zmod(z - 1), y)
    y_up, y_down, y_far = at(z, ymod(y + 1)), at(z, ymod(y - 1)), at(z, ymod(y + 2))
    mates = [{"loop": lax.rem(me + d, NL)} for d in range(1, NL)]

    barrier = pltpu.get_barrier_semaphore()
    everyone = [z_up, z_down, y_up, y_down, y_far] + mates
    for other in everyone:
        pl.semaphore_signal(barrier, inc=1, device_id=other, device_id_type=MESH)

    tiles_in = pltpu.make_async_copy(tiles_hbm, tiles.at[pl.ds(0, SLOTS)], local_sems.at[0])
    tiles_in.start()
    own_in = []
    for c in range(CH):
        copy = pltpu.make_async_copy(
            features.at[:, pl.ds(c * FC, FC)], held[0][c].at[rep], local_sems.at[1 + c]
        )
        copy.start()
        own_in.append(copy)
    pl.semaphore_wait(barrier, len(everyone))

    sent = []
    counter = [0]

    def fresh():
        counter[0] += 1
        return counter[0] - 1

    def send(ref, device, sem):
        copy = pltpu.make_async_remote_copy(
            src_ref=ref,
            dst_ref=ref,
            send_sem=send_sems.at[sem],
            recv_sem=recv_sems.at[sem],
            device_id=device,
            device_id_type=MESH,
        )
        copy.start()
        sent.append(copy)

    def landed(ref, sem):
        pltpu.make_async_remote_copy(
            src_ref=ref,
            dst_ref=ref,
            send_sem=send_sems.at[sem],
            recv_sem=recv_sems.at[sem],
            device_id=z_up,
            device_id_type=MESH,
        ).wait_recv()

    def drain():
        for copy in sent:
            copy.wait_send()
        sent.clear()

    half = NZ // 2

    def gather(k, c):
        h = held[k][c]
        sems = {}

        def sem(*name):
            if name not in sems:
                sems[name] = fresh()
            return sems[name]

        def part_a(off, far=0):
            base = pl.multiple_of(zmod(z + off) * NY, NY)
            if far == 0:
                return h.at[pl.ds(base, NY), pl.ds(0, RA), :]
            return h.at[pl.ds(base + (NY // 2) * (far - 1), NY // 2), pl.ds(0, RA), :]

        def part_b(off, dy=0, far=0):
            block = zmod(z + off) * NY + ymod(y + dy)
            cut = 48 if c == 0 else 32
            if far == 0:
                return h.at[block, pl.ds(RA, RB), :]
            if far == 1:
                return h.at[block, pl.ds(RA, cut), :]
            return h.at[block, pl.ds(RA + cut, RB - cut), :]

        def z_send(part, name, i):
            up = half if i == half else 0
            send(part(-(i - 1), far=1 if up else 0), z_up, sem(name, "up", i))
            send(part(i - 1, far=2 if up else 0), z_down, sem(name, "down", i))

        def z_landed(part, name, i):
            far = i == half
            landed(part(-i, far=1 if far else 0), sem(name, "up", i))
            landed(part(i, far=2 if far else 0), sem(name, "down", i))

        def y_send(off):
            send(part_b(off), y_up, sem("yb", "up", off))
            send(part_b(off), y_down, sem("yb", "down", off))

        def y_relay(off):
            landed(part_b(off, -1), sem("yb", "up", off))
            landed(part_b(off, 1), sem("yb", "down", off))
            if off % 2 == 0:
                send(part_b(off, -1), y_up, sem("yb", "far", off))
            else:
                send(part_b(off, 1), y_down, sem("yb", "far", off))

        def y_end(off):
            landed(part_b(off, 2), sem("yb", "far", off))

        def offs(i):
            if i < 0:
                return ()
            return (0,) if i == 0 else ((half,) if i == half else (-i, i))

        z_send(part_b, "zb", 1)
        own_a = h.at[rep, pl.ds(0, RA), :]
        send(own_a, y_up, sem("ya", 1))
        send(own_a, y_down, sem("ya", 3))
        send(own_a, y_far, sem("ya", 2))
        y_send(0)
        yield
        for d in (1, 3, 2):
            landed(h.at[z * NY + ymod(y - d), pl.ds(0, RA), :], sem("ya", d))
        z_send(part_a, "za", 1)
        yield
        for i in range(1, half + 3):
            if i <= half:
                z_landed(part_b, "zb", i)
                if i < half:
                    z_send(part_b, "zb", i + 1)
                for off in offs(i):
                    y_send(off)
                z_landed(part_a, "za", i)
                if i < half:
                    z_send(part_a, "za", i + 1)
            if i - 1 <= half:
                for off in offs(i - 1):
                    y_relay(off)
            for off in offs(i - 2):
                y_end(off)
            yield

    def multiply(k, c, first, count):
        h, total = held[k][c], runs[c]

        def pair(p):
            a, b = 2 * p, 2 * p + 1
            left = jnp.concatenate([tiles[table[0, a]], tiles[table[0, b]]], axis=1)
            right = jnp.concatenate([h[table[1, a]], h[table[1, b]]], axis=0)
            return jnp.dot(left, right, preferred_element_type=jnp.float32)

        def step(i, unused):
            p = first + 2 * i
            one, two = pair(p), pair(p + 1)
            one = jnp.where(table[2, p] > 0, total[p], 0.0) + one
            total[p + 1] = one
            total[p + 2] = jnp.where(table[2, p + 1] > 0, one, 0.0) + two
            return unused

        lax.fori_loop(0, count // 2, step, 0)

    def box(k, c, d):
        return ((k * CH + c) * NL + d)

    def destination(c, d):
        j = lax.rem(me + d, NL)
        end = table[3, j]
        return jnp.where(end >= 0, runs[c][jnp.maximum(end, 0) + 1], 0.0)

    def scatter(k, c):
        base = [fresh() for _ in range(NL - 1)]
        for d in (4, 3, 5, 2, 6, 1, 7):
            outbox[box(k, c, d)] = destination(c, d).astype(jnp.bfloat16)
            copy = pltpu.make_async_remote_copy(
                src_ref=outbox.at[box(k, c, d)],
                dst_ref=inbox.at[box(k, c, d)],
                send_sem=send_sems.at[base[d - 1]],
                recv_sem=recv_sems.at[base[d - 1]],
                device_id=mates[d - 1],
                device_id_type=MESH,
            )
            copy.start()
            sent.append(copy)
        own_sum[c] = destination(c, 0)
        return base

    def collect(k, c, base):
        total = own_sum[c]
        for d in (1, 7, 2, 6, 3, 5, 4):
            landed(inbox.at[box(k, c, d)], base[d - 1])
            total = total + inbox[box(k, c, d)].astype(jnp.float32)
        return jnp.dot(
            total.astype(jnp.bfloat16),
            weights[k, pl.ds(c * FC, FC), :],
            preferred_element_type=jnp.float32,
        )

    def tables():
        tiles[SLOTS] = jnp.zeros((B, B), jnp.bfloat16)
        for c in range(CH):
            runs[c][0] = jnp.zeros((B, FC), jnp.float32)
        for i, row in enumerate(order_tables(dst_ref[...], src_ref[...], count_ref[0])):
            table_v[pl.ds(i, 1), :] = row
        copy = pltpu.make_async_copy(table_v, table, local_sems.at[3])
        copy.start()
        return copy

    table_in = None
    for k in range(LAYERS):
        first, second = gather(k, 0), gather(k, 1)
        if k == 0:
            own_in[0].wait()
        next(first)
        if k == 0:
            own_in[1].wait()
            table_in = tables()
        for _ in range(LAG):
            next(first)
        live = True
        while True:
            try:
                next(first)
            except StopIteration:
                break
            next(second)
        if k == 0:
            tiles_in.wait()
            table_in.wait()
        share = 2 * -(-PAIRS // (2 * LAG))
        done = 0
        for _ in second:
            take = min(share, PAIRS - done)
            if take > 0:
                multiply(k, 0, done, take)
                done += take
        if done < PAIRS:
            multiply(k, 0, done, PAIRS - done)
        base0 = scatter(k, 0)
        multiply(k, 1, 0, PAIRS)
        base1 = scatter(k, 1)
        mixed = collect(k, 0, base0)
        drain()
        mixed = mixed + collect(k, 1, base1) + biases[pl.ds(k, 1), :]
        hidden = jnp.maximum(mixed, 0.0).astype(jnp.bfloat16)
        if k + 1 < LAYERS:
            for c in range(CH):
                held[k + 1][c][rep] = hidden[:, c * FC : (c + 1) * FC]
        else:
            out[...] = hidden
    drain()


def body(features, tiles, tile_dst, tile_src, tile_count, weights, biases):
    vmem, anyspace = pl.BlockSpec(memory_space=pltpu.VMEM), pl.BlockSpec(memory_space=pl.ANY)
    smem = pl.BlockSpec(memory_space=pltpu.SMEM)
    block = pltpu.VMEM((NREP, B, FC), jnp.bfloat16)
    return pl.pallas_call(
        kernel,
        out_shape=jax.ShapeDtypeStruct((B, F), jnp.bfloat16),
        in_specs=[anyspace, anyspace, vmem, vmem, smem, vmem, vmem],
        out_specs=vmem,
        scratch_shapes=[
            block,
            block,
            block,
            block,
            pltpu.VMEM((SLOTS + 1, B, B), jnp.bfloat16),
            pltpu.VMEM((8, B), jnp.int32),
            pltpu.SMEM((8, B), jnp.int32),
            pltpu.VMEM((PAIRS + 1, B, FC), jnp.float32),
            pltpu.VMEM((PAIRS + 1, B, FC), jnp.float32),
            pltpu.VMEM((LAYERS * CH * NL, B, FC), jnp.bfloat16),
            pltpu.VMEM((LAYERS * CH * NL, B, FC), jnp.bfloat16),
            pltpu.VMEM((CH, B, FC), jnp.float32),
            pltpu.SemaphoreType.DMA((LAYERS * CH * NSEM,)),
            pltpu.SemaphoreType.DMA((LAYERS * CH * NSEM,)),
            pltpu.SemaphoreType.DMA((4,)),
        ],
        compiler_params=pltpu.CompilerParams(
            collective_id=0, has_side_effects=True, vmem_limit_bytes=48 * 1024 * 1024
        ),
        cost_estimate=pl.CostEstimate(flops=2 * LAYERS * SLOTS * B * B * F, bytes_accessed=4 << 20, transcendentals=0),
    )(
        features,
        tiles,
        tile_dst.reshape(1, SLOTS),
        tile_src.reshape(1, SLOTS),
        tile_count,
        weights,
        biases,
    )


def solution(mesh):
    in_specs = (
        P(("rep", "loop"), None),
        P(("rep", "loop"), None, None),
        P(("rep", "loop")),
        P(("rep", "loop")),
        P(("rep", "loop")),
        P(),
        P(),
    )
    out_specs = P(("rep", "loop"), None)
    return jax.shard_map(body, mesh=mesh, in_specs=in_specs, out_specs=out_specs, check_vma=False)
```

```python
import jax
import jax.numpy as jnp
from jax import lax
from jax.experimental import pallas as pl
from jax.experimental.pallas import tpu as pltpu
from jax.sharding import PartitionSpec as P

MESH = pl.DeviceIdType.MESH
NZ, NY, NL = 16, 4, 8
NREP = NZ * NY
B = 128
F = 256
SLOTS = 96
LAYERS = 2
RA = 48
RB = B - RA
CUT = 48
VMEM = 62 * 1024 * 1024
HALF = NZ // 2
PAIRS = (SLOTS + NL) // 2
ZB, ZA = 0, 2 * (HALF + 1)
YA = ZA + NY * 2 * (HALF + 1)
YB = YA + NY
RS = YB + 3 * NZ
NSEM = RS + NL


def order_tables(dst, src, count):
    n = SLOTS
    i32 = jnp.int32
    row = lax.broadcasted_iota(i32, (n, n), 0)
    col = lax.broadcasted_iota(i32, (n, n), 1)
    eye = row == col
    lane = lax.broadcasted_iota(i32, (1, n), 1)
    key_row = jnp.where(lane < count, dst, NL)
    key_col = jnp.sum(jnp.where(eye, key_row, 0), axis=1, keepdims=True)
    src_col = jnp.sum(jnp.where(eye, src, 0), axis=1, keepdims=True)
    rank = jnp.sum(jnp.where((key_col == key_row) & (col < row), 1, 0), axis=1, keepdims=True)
    lanes = lax.broadcasted_iota(i32, (n, B), 1)
    onehot = key_col == lanes
    number = jnp.sum(jnp.where(onehot, 1, 0), axis=0, keepdims=True)
    lane_b = lax.broadcasted_iota(i32, (1, B), 1)
    number = jnp.where(lane_b < NL, number, 0)
    pairs = (number + 1) // 2
    row_b = lax.broadcasted_iota(i32, (B, B), 0)
    col_b = lax.broadcasted_iota(i32, (B, B), 1)
    pairs_col = jnp.sum(jnp.where(row_b == col_b, pairs, 0), axis=1, keepdims=True)
    first = jnp.sum(jnp.where(row_b < col_b, pairs_col, 0), axis=0, keepdims=True)
    first_col = jnp.sum(jnp.where(row_b == col_b, first, 0), axis=1, keepdims=True)
    start = jnp.sum(jnp.where(onehot, first, 0), axis=1, keepdims=True)
    place = jnp.where(key_col < NL, 2 * start + rank, B)
    here = place == lanes
    slot_col = lax.broadcasted_iota(i32, (n, B), 0)
    slot = SLOTS + jnp.sum(jnp.where(here, slot_col - SLOTS, 0), axis=0, keepdims=True)
    source = jnp.sum(jnp.where(here, src_col, 0), axis=0, keepdims=True)
    opens = jnp.sum(jnp.where((first_col == col_b) & (pairs_col > 0), 1, 0), axis=0, keepdims=True)
    last = jnp.where(pairs > 0, first + pairs - 1, -1)
    return slot, source, 1 - opens, last


def kernel(
    features,
    tiles_hbm,
    dst_hbm,
    src_hbm,
    count_ref,
    weights_hbm,
    biases_hbm,
    out,
    h0,
    h1,
    tiles,
    dst_ref,
    src_ref,
    weights,
    biases,
    table_v,
    table,
    runs,
    outbox,
    inbox,
    send_sems,
    recv_sems,
    local_sems,
):
    rep = lax.axis_index("rep")
    me = lax.axis_index("loop")
    z = rep // NY
    y = rep % NY
    held = (h0, h1)

    def zmod(v):
        return lax.rem(v + 2 * NZ, NZ)

    def ymod(v):
        return lax.rem(v + 2 * NY, NY)

    def at(zz, yy):
        return {"rep": zz * NY + yy}

    z_up, z_down = at(zmod(z + 1), y), at(zmod(z - 1), y)
    y_up, y_down, y_far = at(z, ymod(y + 1)), at(z, ymod(y - 1)), at(z, ymod(y + 2))
    mates = [{"loop": lax.rem(me + d, NL)} for d in range(1, NL)]

    barrier = pltpu.get_barrier_semaphore()
    everyone = [z_up, z_down, y_up, y_down, y_far] + mates
    for other in everyone:
        pl.semaphore_signal(barrier, inc=1, device_id=other, device_id_type=MESH)

    copies = [
        pltpu.make_async_copy(a, b, local_sems.at[i])
        for i, (a, b) in enumerate(
            (
                (features, h0.at[rep]),
                (dst_hbm, dst_ref),
                (src_hbm, src_ref),
                (tiles_hbm, tiles.at[pl.ds(0, SLOTS)]),
                (weights_hbm, weights),
                (biases_hbm, biases),
            )
        )
    ]
    for copy in copies:
        copy.start()
    own_in, dst_in, src_in, *later_in = copies
    table_in = pltpu.make_async_copy(table_v, table, local_sems.at[len(copies)])
    pl.semaphore_wait(barrier, len(everyone))

    def tables():
        tiles[SLOTS] = jnp.zeros((B, B), jnp.bfloat16)
        runs[0] = jnp.zeros((B, F), jnp.float32)
        dst_in.wait()
        src_in.wait()
        table_v[...] = jnp.zeros_like(table_v)
        for i, row in enumerate(order_tables(dst_ref[...], src_ref[...], count_ref[0])):
            table_v[pl.ds(i, 1), :] = row
        table_in.start()

    def gather(k, meanwhile):
        h = held[k]

        def link(src, dst, sem, device):
            return pltpu.make_async_remote_copy(
                src_ref=src,
                dst_ref=dst,
                send_sem=send_sems.at[k * NSEM + sem],
                recv_sem=recv_sems.at[k * NSEM + sem],
                device_id=device,
                device_id_type=MESH,
            )

        def send(ref, sem, device):
            link(ref, ref, sem, device).start()

        def landed(ref, sem):
            link(ref, ref, sem, z_up).wait_recv()

        def gone(ref, sem):
            link(ref, ref, sem, z_up).wait_send()

        def block(off, dy):
            return zmod(z + off) * NY + ymod(y + dy)

        def rows_a(off, dy):
            return h.at[block(off, dy), pl.ds(0, RA), :]

        def rows_b(off, dy=0, up=None):
            if up is None:
                return h.at[block(off, dy), pl.ds(RA, RB), :]
            return h.at[block(off, dy), pl.ds(RA, CUT) if up else pl.ds(RA + CUT, RB - CUT), :]

        def sem_zb(up, i):
            return ZB + (0 if up else HALF + 1) + i

        def sem_za(dy, up, i):
            return ZA + (2 * dy + (0 if up else 1)) * (HALF + 1) + i

        def sem_yb(way, off):
            return YB + way * NZ + zmod(off)

        def hop_b(do, i, last=False):
            for up in (True, False):
                off = -i if up else i
                do(rows_b(off, up=up if last else None), sem_zb(up, i), up)

        def hop_a(do, dy, i, last=False):
            for up in (True, False):
                if not last or up == (dy < 2):
                    do(rows_a(-i if up else i, dy), sem_za(dy, up, i), up)

        def forward(ref_of, dy, i, last):
            def do(unused, sem, up):
                off = -(i - 1) if up else i - 1
                if dy is None:
                    ref = rows_b(off, up=up if last else None)
                else:
                    ref = rows_a(off, dy)
                send(ref, sem, z_up if up else z_down)

            return do

        def send_b(i, last=False):
            hop_b(forward(rows_b, None, i, last), i, last)

        def send_a(dy, i, last=False):
            hop_a(forward(rows_a, dy, i, last), dy, i, last)

        def wait(ref, sem, up):
            landed(ref, sem)

        def y_send(off):
            send(rows_b(off), sem_yb(0, off), y_up)
            send(rows_b(off), sem_yb(1, off), y_down)

        def y_relay(off, parity):
            landed(rows_b(off, -1), sem_yb(0, off))
            landed(rows_b(off, 1), sem_yb(1, off))
            way = 1 - 2 * parity
            send(rows_b(off, -way), sem_yb(2, off), at(z, ymod(y + way)))

        def y_end(off):
            landed(rows_b(off, 2), sem_yb(2, off))

        others = (3, 1, 2)
        own_a = rows_a(0, 0)
        send_b(1)
        send_a(0, 1)
        for dy, device in ((1, y_up), (3, y_down), (2, y_far)):
            send(own_a, YA + dy, device)
        y_send(0)
        meanwhile()
        hop_b(wait, 1)
        send_b(2)
        y_send(-1)
        y_send(1)
        hop_a(wait, 0, 1)
        send_a(0, 2)
        for dy in others:
            landed(rows_a(0, dy), YA + NY - dy)
            send_a(dy, 1)
        y_relay(0, 0)

        def middle(i, unused):
            hop_b(wait, i)
            send_b(i + 1)
            y_send(-i)
            y_send(i)
            hop_a(wait, 0, i)
            send_a(0, i + 1)
            for dy in others:
                hop_a(wait, dy, i - 1)
                send_a(dy, i)
            y_relay(-(i - 1), lax.rem(i - 1, 2))
            y_relay(i - 1, lax.rem(i - 1, 2))
            return unused

        lax.fori_loop(2, HALF - 1, middle, 0)
        i = HALF - 1
        hop_b(wait, i)
        send_b(HALF, True)
        y_send(-i)
        y_send(i)
        hop_a(wait, 0, i)
        send_a(0, HALF, True)
        for dy in others:
            hop_a(wait, dy, i - 1)
            send_a(dy, i)
        y_relay(-(i - 1), (i - 1) % 2)
        y_relay(i - 1, (i - 1) % 2)
        i = HALF
        hop_b(wait, i, True)
        y_send(i)
        for dy in others:
            hop_a(wait, dy, i - 1)
            send_a(dy, i, True)
        y_relay(-(i - 1), (i - 1) % 2)
        y_relay(i - 1, (i - 1) % 2)
        hop_a(wait, 0, i, True)
        y_relay(i, i % 2)
        for dy in others:
            hop_a(wait, dy, i, True)

        def arrive(off, unused):
            y_end(off)
            return unused

        lax.fori_loop(0, NZ, arrive, 0)

        def drain():
            def sent(ref, sem, up):
                gone(ref, sem)

            def hops(i, unused):
                hop_b(sent, i)
                for dy in range(NY):
                    hop_a(sent, dy, i)
                return unused

            lax.fori_loop(1, HALF, hops, 0)
            hop_b(sent, HALF, True)
            for dy in range(NY):
                hop_a(sent, dy, HALF, True)
            for dy in others:
                gone(own_a, YA + dy)

            def ways(j, unused):
                gone(rows_b(0), YB + j)
                return unused

            lax.fori_loop(0, 3 * NZ, ways, 0)

        return drain

    def multiply(k):
        h = held[k]

        def pair(p):
            a, b = 2 * p, 2 * p + 1
            left = jnp.concatenate([tiles[table[0, a]], tiles[table[0, b]]], axis=1)
            right = jnp.concatenate([h[table[1, a]], h[table[1, b]]], axis=0)
            return jnp.dot(left, right, preferred_element_type=jnp.float32)

        def step(i, unused):
            for p in (2 * i, 2 * i + 1):
                runs[p + 1] = jnp.where(table[2, p] > 0, runs[p], 0.0) + pair(p)
            return unused

        lax.fori_loop(0, PAIRS // 2, step, 0)

    def destination(d):
        end = table[3, lax.rem(me + d, NL)]
        return jnp.where(end >= 0, runs[jnp.maximum(end, 0) + 1], 0.0)

    def partial_copy(k, d):
        return pltpu.make_async_remote_copy(
            src_ref=outbox.at[k * NL + d],
            dst_ref=inbox.at[k * NL + d],
            send_sem=send_sems.at[k * NSEM + RS + d],
            recv_sem=recv_sems.at[k * NSEM + RS + d],
            device_id=mates[d - 1],
            device_id_type=MESH,
        )

    def reduce(k, meanwhile):
        for d in (4, 3, 5, 2, 6, 1, 7):
            outbox[k * NL + d] = destination(d).astype(jnp.bfloat16)
            partial_copy(k, d).start()
        meanwhile()
        total = destination(0)
        for d in (1, 7, 2, 6, 3, 5, 4):
            partial_copy(k, d).wait_recv()
            total = total + inbox[k * NL + d].astype(jnp.float32)
        return total.astype(jnp.bfloat16)

    own_in.wait()
    drain = None
    for k in range(LAYERS):
        drain = gather(k, tables if k == 0 else drain)
        if k == 0:
            table_in.wait()
            for copy in later_in:
                copy.wait()
        multiply(k)
        aggregate = reduce(k, drain if k + 1 == LAYERS else lambda: None)
        mixed = jnp.dot(aggregate, weights[k], preferred_element_type=jnp.float32) + biases[pl.ds(k, 1), :]
        hidden = jnp.maximum(mixed, 0.0).astype(jnp.bfloat16)
        if k + 1 < LAYERS:
            held[k + 1][rep] = hidden
        else:
            out[...] = hidden
    for i in range(LAYERS):
        for d in range(1, NL):
            partial_copy(i, d).wait_send()


def body(features, tiles, tile_dst, tile_src, tile_count, weights, biases):
    vmem, anyspace = pl.BlockSpec(memory_space=pltpu.VMEM), pl.BlockSpec(memory_space=pl.ANY)
    smem = pl.BlockSpec(memory_space=pltpu.SMEM)
    block = pltpu.VMEM((NREP, B, F), jnp.bfloat16)
    return pl.pallas_call(
        kernel,
        out_shape=jax.ShapeDtypeStruct((B, F), jnp.bfloat16),
        in_specs=[anyspace, anyspace, anyspace, anyspace, smem, anyspace, anyspace],
        out_specs=vmem,
        scratch_shapes=[
            block,
            block,
            pltpu.VMEM((SLOTS + 1, B, B), jnp.bfloat16),
            pltpu.VMEM((1, SLOTS), jnp.int32),
            pltpu.VMEM((1, SLOTS), jnp.int32),
            pltpu.VMEM((LAYERS, F, F), jnp.bfloat16),
            pltpu.VMEM((LAYERS, F), jnp.float32),
            pltpu.VMEM((8, B), jnp.int32),
            pltpu.SMEM((8, B), jnp.int32),
            pltpu.VMEM((PAIRS + 1, B, F), jnp.float32),
            pltpu.VMEM((LAYERS * NL, B, F), jnp.bfloat16),
            pltpu.VMEM((LAYERS * NL, B, F), jnp.bfloat16),
            pltpu.SemaphoreType.DMA((LAYERS * NSEM,)),
            pltpu.SemaphoreType.DMA((LAYERS * NSEM,)),
            pltpu.SemaphoreType.DMA((8,)),
        ],
        compiler_params=pltpu.CompilerParams(
            collective_id=0, has_side_effects=True, vmem_limit_bytes=VMEM
        ),
        cost_estimate=pl.CostEstimate(flops=2 * LAYERS * SLOTS * B * B * F, bytes_accessed=4 << 20, transcendentals=0),
    )(
        features,
        tiles,
        tile_dst.reshape(1, SLOTS),
        tile_src.reshape(1, SLOTS),
        tile_count,
        weights,
        biases,
    )


def solution(mesh):
    in_specs = (
        P(("rep", "loop"), None),
        P(("rep", "loop"), None, None),
        P(("rep", "loop")),
        P(("rep", "loop")),
        P(("rep", "loop")),
        P(),
        P(),
    )
    out_specs = P(("rep", "loop"), None)
    return jax.shard_map(body, mesh=mesh, in_specs=in_specs, out_specs=out_specs, check_vma=False)
```

```python
import jax
import jax.numpy as jnp
from jax import lax
from jax.experimental import pallas as pl
from jax.experimental.pallas import tpu as pltpu
from jax.sharding import PartitionSpec as P

MESH = pl.DeviceIdType.MESH
NZ, NY, NL = 16, 4, 8
NREP = NZ * NY
B = 128
F = 256
SLOTS = 96
LAYERS = 2
RA = 48
RB = B - RA
CUT = 48
VMEM = 62 * 1024 * 1024
HALF = NZ // 2
CELLS = NL * NREP
ZB, ZA = 0, 2 * (HALF + 1)
YA = ZA + NY * 2 * (HALF + 1)
YB = YA + NY
RS = YB + 3 * NZ
NSEM = RS + NL
ORDER = (
    ("zb", 0, 1), ("zb", 1, 1), ("za", 0, 0, 1), ("ya", 3), ("ya", 1), ("za", 0, 1, 1), ("zb", 0, 2), ("zb", 1, 2),
    ("yo", 0), ("za", 3, 0, 1), ("ya", 2), ("yr", 15), ("za", 3, 1, 1), ("za", 1, 1, 1), ("za", 1, 0, 1), ("yr", 0),
    ("za", 0, 0, 2), ("za", 0, 1, 2), ("zb", 1, 3), ("zb", 0, 3), ("za", 2, 0, 1), ("za", 3, 1, 2), ("za", 3, 0, 2),
    ("yo", 14), ("yr", 1), ("za", 2, 1, 1), ("za", 1, 0, 2), ("yo", 2), ("za", 1, 1, 2), ("yo", 15), ("yr", 2),
    ("za", 0, 0, 3), ("za", 0, 1, 3), ("yr", 14), ("yr", 13), ("zb", 0, 4), ("zb", 1, 4), ("za", 2, 1, 2),
    ("za", 3, 0, 3), ("za", 3, 1, 3), ("za", 1, 0, 3), ("za", 1, 1, 3), ("ye", 15), ("za", 2, 0, 2), ("yr", 3),
    ("g", 15), ("za", 0, 0, 4), ("ye", 0), ("za", 0, 1, 4), ("ye", 1), ("yo", 1), ("yo", 13), ("zb", 0, 5),
    ("zb", 1, 5), ("za", 3, 1, 4), ("za", 3, 0, 4), ("ye", 2), ("g", 0), ("za", 2, 0, 3), ("za", 1, 0, 4),
    ("za", 1, 1, 4), ("g", 1), ("ye", 13), ("za", 2, 1, 3), ("za", 0, 0, 5), ("yr", 12), ("ye", 14), ("yr", 4),
    ("za", 0, 1, 5), ("zb", 0, 6), ("zb", 1, 6), ("g", 14), ("yo", 5), ("yo", 3), ("za", 1, 0, 5), ("za", 3, 1, 5),
    ("yo", 4), ("za", 3, 0, 5), ("za", 2, 0, 4), ("ye", 3), ("za", 2, 1, 4), ("za", 1, 1, 5), ("yr", 5),
    ("za", 0, 0, 6), ("g", 13), ("ye", 12), ("zb", 1, 7), ("za", 0, 1, 6), ("g", 3), ("zb", 0, 7), ("za", 3, 0, 6),
    ("g", 2), ("za", 2, 0, 5), ("za", 3, 1, 6), ("za", 2, 1, 5), ("ye", 4), ("yr", 11), ("yo", 12), ("za", 1, 0, 6),
    ("za", 0, 0, 7), ("yo", 11), ("yr", 6), ("za", 1, 1, 6), ("yo", 10), ("yo", 6), ("yr", 9), ("g", 12),
    ("za", 3, 0, 7), ("za", 2, 0, 6), ("zb", 2, 8), ("yr", 10), ("za", 2, 1, 6), ("za", 0, 1, 7), ("za", 3, 1, 7),
    ("yr", 7), ("za", 1, 1, 7), ("yo", 7), ("ye", 11), ("ye", 6), ("ye", 5), ("g", 11), ("g", 5), ("g", 4),
    ("za", 1, 0, 7), ("za", 2, 0, 7), ("yr", 8), ("ye", 10), ("yo", 8), ("yo", 9), ("za", 3, 0, 8), ("za", 0, 1, 8),
    ("ye", 7), ("ye", 9), ("za", 2, 1, 7), ("g", 10), ("g", 6), ("g", 7), ("g", 9), ("za", 1, 1, 8), ("za", 2, 0, 8),
    ("ye", 8), ("g", 8),
)
MIRROR = True
LATE = 0


def order_tables(dst, src, count):
    n = SLOTS
    i32 = jnp.int32
    row = lax.broadcasted_iota(i32, (n, n), 0)
    col = lax.broadcasted_iota(i32, (n, n), 1)
    lane = lax.broadcasted_iota(i32, (1, n), 1)
    key_row = jnp.where(lane < count, dst * NREP + src, CELLS)
    key = jnp.sum(jnp.where(row == col, key_row, 0), axis=1, keepdims=True)
    before = (key_row < key) | ((key_row == key) & (col < row))
    place = jnp.sum(jnp.where(before, 1, 0), axis=1, keepdims=True)
    lanes = lax.broadcasted_iota(i32, (n, B), 1)
    slot = lax.broadcasted_iota(i32, (n, B), 0)
    rows = []
    for part in range(CELLS // B):
        last = jnp.max(jnp.where(key == lanes + part * B, place, -1), axis=0, keepdims=True)
        rows.append(jnp.where(last < 0, SLOTS, last))
    here = place == lanes
    rows.append(jnp.sum(jnp.where(here, slot, 0), axis=0, keepdims=True))
    mine = jnp.sum(jnp.where(here, key, 0), axis=0, keepdims=True)
    prior = jnp.sum(jnp.where(place + 1 == lanes, key, 0), axis=0, keepdims=True)
    rows.append(jnp.where((mine == prior) & (lanes[:1] > 0), 1, 0))
    return rows


def kernel(
    features,
    tiles_hbm,
    dst_hbm,
    src_hbm,
    count_ref,
    weights_hbm,
    biases_hbm,
    out,
    held,
    tiles,
    merged,
    dst_ref,
    src_ref,
    weights,
    biases,
    table_v,
    table,
    total,
    outbox,
    inbox,
    sent_sems,
    recv_sems,
    local_sems,
):
    rep = lax.axis_index("rep")
    me = lax.axis_index("loop")
    z = rep // NY
    y = rep % NY
    face = 1 - 2 * (lax.rem(z, 4) // 2) if MIRROR else 1

    def zmod(v):
        return lax.rem(v + 2 * NZ, NZ)

    def ymod(v):
        return lax.rem(v + 2 * NY, NY)

    def at(zz, yy):
        return {"rep": zz * NY + yy}

    y_up, y_down, y_far = at(z, ymod(y + 1)), at(z, ymod(y - 1)), at(z, ymod(y + 2))
    mates = [{"loop": lax.rem(me + d, NL)} for d in range(1, NL)]

    barrier = pltpu.get_barrier_semaphore()
    everyone = [at(zmod(z + 1), y), at(zmod(z - 1), y), y_up, y_down, y_far] + mates
    for other in everyone:
        pl.semaphore_signal(barrier, inc=1, device_id=other, device_id_type=MESH)

    copies = [
        pltpu.make_async_copy(a, b, local_sems.at[i])
        for i, (a, b) in enumerate(
            (
                (features, held.at[rep]),
                (dst_hbm, dst_ref),
                (src_hbm, src_ref),
                (tiles_hbm, tiles),
                (weights_hbm, weights),
                (biases_hbm, biases),
            )
        )
    ]
    for copy in copies:
        copy.start()
    own_in, dst_in, src_in, tiles_in, *later_in = copies
    table_in = pltpu.make_async_copy(table_v, table, local_sems.at[len(copies)])

    def tables():
        merged[SLOTS] = jnp.zeros((B, B), jnp.bfloat16)
        dst_in.wait()
        src_in.wait()
        table_v[...] = jnp.zeros_like(table_v)
        for i, row in enumerate(order_tables(dst_ref[...], src_ref[...], count_ref[0])):
            table_v[pl.ds(i, 1), :] = row
        table_in.start()
        tiles_in.wait()
        table_in.wait()

    def merge():
        def step(i, run):
            for q in range(4):
                q = 4 * i + q
                run = jnp.where(table[5, q] > 0, run, 0.0) + tiles[table[4, q]].astype(jnp.float32)
                merged[q] = run.astype(jnp.bfloat16)
            return run

        lax.fori_loop(0, SLOTS // 4, step, jnp.zeros((B, B), jnp.float32))

    def partial_copy(k, d):
        return pltpu.make_async_remote_copy(
            src_ref=outbox.at[k * NL + d],
            dst_ref=inbox.at[k * NL + d],
            send_sem=sent_sems.at[LAYERS + k],
            recv_sem=recv_sems.at[k * NSEM + RS + d],
            device_id=mates[d - 1],
            device_id_type=MESH,
        )

    def layer(k, unused):
        def link(ref, sem, device):
            return pltpu.make_async_remote_copy(
                src_ref=ref,
                dst_ref=ref,
                send_sem=sent_sems.at[k],
                recv_sem=recv_sems.at[k * NSEM + sem],
                device_id=device,
                device_id_type=MESH,
            )

        def send(ref, sem, device):
            link(ref, sem, device).start()

        def landed(ref, sem):
            link(ref, sem, y_up).wait_recv()

        def block(off, dy):
            return k * NREP + zmod(z + off) * NY + ymod(y + dy)

        def rows_a(off, dy):
            return held.at[block(off, dy), pl.ds(0, RA), :]

        def rows_b(off, dy=0, part=None):
            if part is None:
                return held.at[block(off, dy), pl.ds(RA, RB), :]
            return held.at[block(off, dy), pl.ds(RA, CUT) if part else pl.ds(RA + CUT, RB - CUT), :]

        def sem_zb(way, i):
            return ZB + (1 - way) // 2 * (HALF + 1) + i

        def sem_za(dy, way, i):
            return ZA + (2 * dy + (1 - way) // 2) * (HALF + 1) + i

        def send_b(way, i):
            ref = rows_b(-way * (i - 1), 0, None if i < HALF else way > 0)
            send(ref, sem_zb(way, i), at(zmod(z + way), y))

        def send_a(dy, way, i):
            send(rows_a(-way * (i - 1), dy), sem_za(dy, way, i), at(zmod(z + way), y))

        def sem_yb(kind, off):
            return YB + kind * NZ + zmod(off)

        def y_send(off):
            send(rows_b(off), sem_yb(0, off), y_up)
            send(rows_b(off), sem_yb(1, off), y_down)

        def turned(off):
            off = off if off <= HALF else off - NZ
            return off * face if abs(off) < HALF - 1 else off

        def from_y(off, up):
            landed(rows_b(off, -1 if up else 1), sem_yb(0 if up else 1, off))

        def group(off):
            zz = zmod(z + off) * NY
            right = held[pl.ds(k * NREP + zz, NY)].reshape(NY * B, F)

            def product(d):
                cell = lax.rem(me + d, NL) * NREP + zz
                line, at0 = cell // B, lax.rem(cell, B)
                left = jnp.concatenate([merged[table[line, at0 + yy]] for yy in range(NY)], axis=1)
                return jnp.dot(left, right, preferred_element_type=jnp.float32)

            return product

        def handle(step):
            kind, *which = step
            if kind == "zb" and which[1] == HALF:
                for way in (1, -1):
                    landed(rows_b(HALF, 0, way > 0), sem_zb(way, HALF))
                y_send(HALF)
            elif kind == "zb":
                up, i = which
                way = (1 if up else -1) * (face if i < HALF - 1 else 1)
                landed(rows_b(-way * i), sem_zb(way, i))
                send_b(way, i + 1)
                y_send(-way * i)
            elif kind == "za":
                dy, up, i = which
                way = (1 if up else -1) * (face if i < HALF - 1 else 1)
                landed(rows_a(-way * i, dy), sem_za(dy, way, i))
                if i < HALF - 1 or (i == HALF - 1 and up == (dy < 2)):
                    send_a(dy, way, i + 1)
            elif kind == "ya":
                dy = which[0]
                landed(rows_a(0, dy), YA + NY - dy)
                send_a(dy, 1, 1)
                send_a(dy, -1, 1)
            elif kind in ("yr", "yo"):
                even = which[0] % 2 == 0
                off = turned(which[0])
                from_y(off, even == (kind == "yr"))
                if kind == "yr":
                    send(rows_b(off, -1 if even else 1), sem_yb(2, off), y_up if even else y_down)
            elif kind == "ye":
                off = turned(which[0])
                landed(rows_b(off, 2), sem_yb(2, off))

        for way in (1, -1):
            send_b(way, 1)
        for way in (1, -1):
            send_a(0, way, 1)
        for dy, device in ((1, y_up), (3, y_down), (2, y_far)):
            send(rows_a(0, 0), YA + dy, device)
        y_send(0)

        @pl.when(k == 0)
        def _():
            tables()
            merge()
            for copy in later_in:
                copy.wait()

        begun = False
        late = []
        final = max(n for n, step in enumerate(ORDER) if step[0] != "g")
        for n, step in enumerate(ORDER):
            if step[0] != "g":
                handle(step)
            elif n > final or n > len(ORDER) - LATE:
                late.append(turned(step[1]))
            else:
                product = group(turned(step[1]))
                for d in range(NL):
                    part = product(d)
                    total[d] = total[d] + part if begun else part
                begun = True
        late = [group(off) for off in late]
        for d in (4, 3, 5, 2, 6, 1, 7, 0):
            part = total[d]
            for product in late:
                part = part + product(d)
            if d:
                outbox[k * NL + d] = part.astype(jnp.bfloat16)
                partial_copy(k, d).start()
        for d in (1, 7, 2, 6, 3, 5, 4):
            partial_copy(k, d).wait_recv()
            part = part + inbox[k * NL + d].astype(jnp.float32)
        mixed = jnp.dot(part.astype(jnp.bfloat16), weights[k], preferred_element_type=jnp.float32)
        hidden = jnp.maximum(mixed + biases[pl.ds(k, 1), :], 0.0).astype(jnp.bfloat16)

        @pl.when(k + 1 < LAYERS)
        def _():
            held[(k + 1) * NREP + rep] = hidden

        @pl.when(k + 1 == LAYERS)
        def _():
            out[...] = hidden

        return unused

    own_in.wait()
    pl.semaphore_wait(barrier, len(everyone))
    lax.fori_loop(0, LAYERS, layer, 0)
    for k in range(LAYERS):
        for buffer, sem, blocks in ((held, k, NREP - 1), (outbox, LAYERS + k, NL - 1)):
            whole = buffer.at[pl.ds(0, blocks)]
            pltpu.make_async_remote_copy(
                src_ref=whole,
                dst_ref=whole,
                send_sem=sent_sems.at[sem],
                recv_sem=recv_sems.at[0],
                device_id=y_up,
                device_id_type=MESH,
            ).wait_send()


def body(features, tiles, tile_dst, tile_src, tile_count, weights, biases):
    vmem, anyspace = pl.BlockSpec(memory_space=pltpu.VMEM), pl.BlockSpec(memory_space=pl.ANY)
    smem = pl.BlockSpec(memory_space=pltpu.SMEM)
    return pl.pallas_call(
        kernel,
        out_shape=jax.ShapeDtypeStruct((B, F), jnp.bfloat16),
        in_specs=[anyspace, anyspace, anyspace, anyspace, smem, anyspace, anyspace],
        out_specs=vmem,
        scratch_shapes=[
            pltpu.VMEM((LAYERS * NREP, B, F), jnp.bfloat16),
            pltpu.VMEM((SLOTS, B, B), jnp.bfloat16),
            pltpu.VMEM((SLOTS + 1, B, B), jnp.bfloat16),
            pltpu.VMEM((1, SLOTS), jnp.int32),
            pltpu.VMEM((1, SLOTS), jnp.int32),
            pltpu.VMEM((LAYERS, F, F), jnp.bfloat16),
            pltpu.VMEM((LAYERS, F), jnp.float32),
            pltpu.VMEM((8, B), jnp.int32),
            pltpu.SMEM((8, B), jnp.int32),
            pltpu.VMEM((NL, B, F), jnp.float32),
            pltpu.VMEM((LAYERS * NL, B, F), jnp.bfloat16),
            pltpu.VMEM((LAYERS * NL, B, F), jnp.bfloat16),
            pltpu.SemaphoreType.DMA((2 * LAYERS,)),
            pltpu.SemaphoreType.DMA((LAYERS * NSEM,)),
            pltpu.SemaphoreType.DMA((8,)),
        ],
        compiler_params=pltpu.CompilerParams(
            collective_id=0, has_side_effects=True, vmem_limit_bytes=VMEM
        ),
        cost_estimate=pl.CostEstimate(flops=2 * LAYERS * CELLS * B * B * F, bytes_accessed=4 << 20, transcendentals=0),
    )(
        features,
        tiles,
        tile_dst.reshape(1, SLOTS),
        tile_src.reshape(1, SLOTS),
        tile_count,
        weights,
        biases,
    )


def solution(mesh):
    in_specs = (
        P(("rep", "loop"), None),
        P(("rep", "loop"), None, None),
        P(("rep", "loop")),
        P(("rep", "loop")),
        P(("rep", "loop")),
        P(),
        P(),
    )
    out_specs = P(("rep", "loop"), None)
    return jax.shard_map(body, mesh=mesh, in_specs=in_specs, out_specs=out_specs, check_vma=False)
```

```python
import jax
import jax.numpy as jnp
from jax import lax
from jax.experimental import pallas as pl
from jax.experimental.pallas import tpu as pltpu
from jax.sharding import PartitionSpec as P

MESH = pl.DeviceIdType.MESH
NZ, NY, NL = 16, 4, 8
NREP = NZ * NY
B = 128
F = 256
SLOTS = 96
LAYERS = 2
RA = 48
RB = B - RA
CUT = 48
VMEM = 62 * 1024 * 1024
HALF = NZ // 2
CELLS = NL * NREP
ZB, ZA = 0, 4 * (HALF + 1)
YA = ZA + NY * 2 * (HALF + 1)
YB = YA + NY
RS = YB + 3 * NZ
NSEM = RS + NL
ORDER = (
    ("s", "ya", 1), ("s", "zb", 1, 1, 0), ("s", "zb", 0, 1, 0), ("s", "zb", 1, 1, 1), ("s", "zb", 0, 1, 1),
    ("s", "za", 0, 0, 1), ("s", "ya", 3), ("s", "za", 0, 1, 1), ("s", "ya", 2), ("w", "zb", 0, 1, 0),
    ("s", "zb", 0, 2, 0), ("w", "zb", 0, 1, 1), ("w", "zb", 1, 1, 0), ("s", "zb", 1, 2, 0), ("s", "zb", 0, 2, 1),
    ("w", "ya", 1), ("s", "za", 3, 0, 1), ("w", "ya", 3), ("s", "yb", 1, 1, 2), ("w", "za", 0, 0, 1),
    ("w", "zb", 1, 1, 1), ("s", "zb", 1, 2, 1), ("s", "yb", 1, 0, 2), ("s", "za", 3, 1, 1), ("w", "za", 0, 1, 1),
    ("s", "za", 1, 0, 1), ("s", "za", 1, 1, 1), ("s", "yb", 0, 1, 2), ("s", "za", 0, 1, 2), ("s", "yb", 1, 15, 2),
    ("s", "za", 0, 0, 2), ("w", "zb", 0, 2, 0), ("s", "zb", 0, 3, 0), ("w", "zb", 1, 2, 0), ("s", "zb", 1, 3, 0),
    ("w", "zb", 0, 2, 1), ("s", "yb", 0, 0, 2), ("s", "zb", 0, 3, 1), ("w", "zb", 1, 2, 1), ("s", "zb", 1, 3, 1),
    ("s", "yb", 0, 14, 2), ("w", "za", 3, 0, 1), ("w", "za", 3, 1, 1), ("s", "za", 3, 0, 2), ("s", "za", 3, 1, 2),
    ("w", "za", 1, 0, 1), ("w", "ya", 2), ("s", "za", 2, 0, 1), ("s", "za", 2, 1, 1), ("w", "yb", 1, 1, 2),
    ("w", "za", 1, 1, 1), ("s", "za", 1, 0, 2), ("s", "za", 1, 1, 2), ("w", "za", 0, 1, 2), ("w", "za", 0, 0, 2),
    ("s", "yb", 0, 2, 2), ("s", "yb", 1, 14, 2), ("w", "zb", 0, 3, 0), ("s", "za", 0, 1, 3), ("s", "zb", 0, 4, 0),
    ("s", "za", 0, 0, 3), ("w", "zb", 1, 3, 0), ("w", "yb", 1, 15, 2), ("s", "yb", 0, 15, 2), ("s", "yb", 2, 15, 2),
    ("s", "zb", 1, 4, 0), ("w", "zb", 1, 3, 1), ("w", "zb", 0, 3, 1), ("s", "zb", 0, 4, 1), ("s", "zb", 1, 4, 1),
    ("w", "za", 3, 1, 2), ("s", "za", 3, 1, 3), ("w", "za", 2, 0, 1), ("s", "za", 2, 0, 2), ("s", "yb", 0, 13, 2),
    ("s", "yb", 2, 1, 2), ("w", "za", 3, 0, 2), ("w", "za", 1, 0, 2), ("s", "za", 3, 0, 3), ("w", "za", 2, 1, 1),
    ("w", "yb", 0, 0, 2), ("s", "za", 2, 1, 2), ("w", "za", 1, 1, 2), ("s", "za", 1, 0, 3), ("s", "yb", 1, 3, 2),
    ("s", "za", 1, 1, 3), ("s", "yb", 1, 13, 2), ("w", "zb", 0, 4, 0), ("s", "zb", 0, 5, 0), ("s", "yb", 2, 0, 2),
    ("w", "zb", 1, 4, 0), ("s", "zb", 1, 5, 0), ("w", "za", 0, 0, 3), ("w", "zb", 0, 4, 1), ("s", "zb", 0, 5, 1),
    ("s", "za", 0, 0, 4), ("s", "yb", 1, 2, 2), ("w", "za", 0, 1, 3), ("w", "zb", 1, 4, 1), ("s", "zb", 1, 5, 1),
    ("s", "za", 0, 1, 4), ("s", "yb", 0, 4, 2), ("w", "za", 2, 0, 2), ("s", "za", 2, 0, 3), ("w", "za", 2, 1, 2),
    ("w", "za", 3, 0, 3), ("s", "za", 2, 1, 3), ("s", "za", 3, 0, 4), ("s", "yb", 0, 3, 2), ("w", "za", 3, 1, 3),
    ("s", "za", 3, 1, 4), ("w", "yb", 0, 2, 2), ("s", "yb", 0, 12, 2), ("w", "za", 1, 0, 3), ("s", "yb", 1, 4, 2),
    ("w", "yb", 0, 14, 2), ("s", "za", 1, 0, 4), ("w", "za", 1, 1, 3), ("s", "za", 1, 1, 4), ("w", "zb", 0, 5, 0),
    ("s", "zb", 0, 6, 0), ("w", "yb", 0, 1, 2), ("w", "zb", 1, 5, 0), ("s", "zb", 1, 6, 0), ("w", "zb", 0, 5, 1),
    ("s", "yb", 1, 12, 2), ("s", "zb", 0, 6, 1), ("s", "yb", 2, 2, 2), ("w", "zb", 1, 5, 1), ("s", "zb", 1, 6, 1),
    ("w", "za", 0, 0, 4), ("w", "yb", 2, 0, 2), ("s", "za", 0, 0, 5), ("s", "yb", 2, 14, 2), ("w", "za", 0, 1, 4),
    ("s", "za", 0, 1, 5), ("w", "yb", 2, 15, 2), ("w", "yb", 1, 3, 2), ("s", "yb", 1, 5, 2), ("s", "yb", 0, 5, 2),
    ("w", "za", 2, 0, 3), ("s", "za", 2, 0, 4), ("w", "za", 2, 1, 3), ("s", "za", 2, 1, 4), ("w", "za", 3, 0, 4),
    ("w", "za", 1, 0, 4), ("s", "za", 1, 0, 5), ("s", "yb", 2, 3, 2), ("w", "za", 3, 1, 4), ("w", "za", 1, 1, 4),
    ("s", "za", 3, 0, 5), ("w", "yb", 0, 12, 2), ("s", "za", 1, 1, 5), ("s", "za", 3, 1, 5), ("s", "yb", 1, 11, 2),
    ("w", "yb", 0, 3, 2), ("w", "zb", 0, 6, 0), ("s", "yb", 2, 12, 2), ("w", "yb", 2, 1, 2), ("w", "yb", 1, 14, 2),
    ("w", "zb", 1, 6, 0), ("s", "zb", 0, 7, 0), ("s", "zb", 1, 7, 0), ("w", "yb", 0, 15, 2), ("w", "zb", 0, 6, 1),
    ("w", "zb", 1, 6, 1), ("s", "yb", 1, 10, 2), ("s", "zb", 0, 7, 1), ("w", "yb", 1, 13, 2), ("s", "zb", 1, 7, 1),
    ("w", "yb", 1, 2, 2), ("s", "yb", 1, 6, 2), ("w", "za", 0, 0, 5), ("s", "yb", 2, 13, 2), ("s", "yb", 0, 6, 2),
    ("w", "za", 2, 0, 4), ("s", "za", 2, 0, 5), ("s", "yb", 0, 10, 2), ("w", "za", 2, 1, 4), ("s", "za", 2, 1, 5),
    ("s", "za", 0, 0, 6), ("g", 15), ("w", "za", 0, 1, 5), ("s", "za", 0, 1, 6), ("w", "yb", 1, 12, 2),
    ("s", "yb", 0, 11, 2), ("w", "yb", 0, 4, 2), ("w", "za", 1, 0, 5), ("s", "za", 1, 0, 6), ("w", "za", 1, 1, 5),
    ("s", "za", 1, 1, 6), ("w", "yb", 1, 5, 2), ("w", "yb", 2, 2, 2), ("g", 2), ("w", "za", 3, 0, 5),
    ("w", "yb", 2, 3, 2), ("s", "za", 3, 0, 6), ("w", "za", 3, 1, 5), ("s", "za", 3, 1, 6), ("s", "yb", 2, 4, 2),
    ("s", "yb", 2, 5, 2), ("w", "zb", 1, 7, 0), ("w", "yb", 1, 4, 2), ("s", "zb", 1, 8, 0), ("w", "zb", 0, 7, 1),
    ("s", "zb", 0, 8, 1), ("g", 3), ("w", "za", 2, 0, 5), ("s", "za", 2, 0, 6), ("w", "zb", 1, 7, 1),
    ("w", "za", 2, 1, 5), ("s", "yb", 1, 9, 2), ("s", "za", 2, 1, 6), ("w", "yb", 0, 6, 2), ("w", "yb", 1, 11, 2),
    ("s", "yb", 0, 9, 2), ("w", "za", 0, 0, 6), ("w", "zb", 0, 7, 0), ("w", "za", 0, 1, 6), ("s", "yb", 1, 7, 2),
    ("s", "yb", 2, 6, 2), ("w", "yb", 1, 0, 2), ("w", "yb", 2, 14, 2), ("s", "za", 0, 1, 7), ("g", 0),
    ("w", "yb", 0, 5, 2), ("w", "za", 1, 1, 6), ("w", "yb", 2, 12, 2), ("w", "za", 1, 0, 6), ("s", "za", 1, 1, 7),
    ("s", "za", 1, 0, 7), ("g", 14), ("w", "za", 3, 1, 6), ("w", "za", 3, 0, 6), ("s", "za", 3, 0, 7),
    ("s", "yb", 2, 11, 2), ("w", "yb", 1, 10, 2), ("w", "yb", 0, 13, 2), ("s", "za", 3, 1, 7), ("w", "yb", 1, 6, 2),
    ("w", "zb", 1, 8, 0), ("w", "yb", 2, 13, 2), ("w", "zb", 0, 8, 1), ("s", "za", 0, 0, 7), ("s", "yb", 0, 8, 2),
    ("s", "yb", 1, 8, 2), ("w", "yb", 0, 10, 2), ("g", 12), ("s", "yb", 2, 10, 2), ("w", "za", 2, 0, 6),
    ("w", "za", 2, 1, 6), ("s", "za", 2, 0, 7), ("w", "yb", 2, 4, 2), ("g", 4), ("w", "yb", 2, 5, 2),
    ("s", "za", 2, 1, 7), ("s", "yb", 0, 7, 2), ("w", "yb", 1, 9, 2), ("s", "yb", 2, 9, 2), ("g", 13), ("g", 5),
    ("w", "za", 0, 1, 7), ("w", "yb", 0, 9, 2), ("w", "yb", 1, 7, 2), ("w", "za", 1, 1, 7), ("s", "za", 1, 1, 8),
    ("s", "za", 0, 1, 8), ("s", "yb", 2, 7, 2), ("w", "yb", 2, 6, 2), ("w", "za", 3, 0, 7), ("s", "za", 3, 0, 8),
    ("w", "za", 1, 0, 7), ("g", 6), ("w", "yb", 0, 8, 2), ("s", "yb", 2, 8, 2), ("w", "za", 2, 0, 7),
    ("s", "za", 2, 0, 8), ("w", "za", 0, 0, 7), ("w", "za", 3, 1, 7), ("w", "yb", 2, 11, 2), ("w", "yb", 0, 11, 2),
    ("g", 1), ("w", "yb", 2, 10, 2), ("g", 10), ("w", "za", 2, 1, 7), ("g", 11), ("w", "yb", 2, 9, 2), ("g", 9),
    ("w", "yb", 0, 7, 2), ("w", "yb", 1, 8, 2), ("w", "za", 3, 0, 8), ("w", "za", 1, 1, 8), ("w", "yb", 2, 7, 2),
    ("g", 7), ("w", "za", 0, 1, 8), ("w", "yb", 2, 8, 2), ("w", "za", 2, 0, 8), ("g", 8),
)


def order_tables(dst, src, count):
    n = SLOTS
    i32 = jnp.int32
    row = lax.broadcasted_iota(i32, (n, n), 0)
    col = lax.broadcasted_iota(i32, (n, n), 1)
    lane = lax.broadcasted_iota(i32, (1, n), 1)
    key_row = jnp.where(lane < count, dst * NREP + src, CELLS)
    key = jnp.sum(jnp.where(row == col, key_row, 0), axis=1, keepdims=True)
    before = (key_row < key) | ((key_row == key) & (col < row))
    place = jnp.sum(jnp.where(before, 1, 0), axis=1, keepdims=True)
    lanes = lax.broadcasted_iota(i32, (n, B), 1)
    slot = lax.broadcasted_iota(i32, (n, B), 0)
    rows = []
    for part in range(CELLS // B):
        last = jnp.max(jnp.where(key == lanes + part * B, place, -1), axis=0, keepdims=True)
        rows.append(jnp.where(last < 0, SLOTS, last))
    here = place == lanes
    rows.append(jnp.sum(jnp.where(here, slot, 0), axis=0, keepdims=True))
    mine = jnp.sum(jnp.where(here, key, 0), axis=0, keepdims=True)
    prior = jnp.sum(jnp.where(place + 1 == lanes, key, 0), axis=0, keepdims=True)
    rows.append(jnp.where((mine == prior) & (lanes[:1] > 0), 1, 0))
    return rows


def kernel(
    features,
    tiles_hbm,
    dst_hbm,
    src_hbm,
    count_ref,
    weights_hbm,
    biases_hbm,
    out,
    held,
    tiles,
    merged,
    dst_ref,
    src_ref,
    weights,
    biases,
    table_v,
    table,
    total,
    outbox,
    inbox,
    sent_sems,
    recv_sems,
    local_sems,
):
    rep = lax.axis_index("rep")
    me = lax.axis_index("loop")
    z = rep // NY
    y = rep % NY
    face = 1 - 2 * (lax.rem(z, 4) // 2)

    def zmod(v):
        return lax.rem(v + 2 * NZ, NZ)

    def ymod(v):
        return lax.rem(v + 2 * NY, NY)

    def at(zz, yy):
        return {"rep": zz * NY + yy}

    y_up, y_down, y_far = at(z, ymod(y + 1)), at(z, ymod(y - 1)), at(z, ymod(y + 2))
    mates = [{"loop": lax.rem(me + d, NL)} for d in range(1, NL)]

    barrier = pltpu.get_barrier_semaphore()
    everyone = [at(zmod(z + 1), y), at(zmod(z - 1), y), y_up, y_down, y_far] + mates
    for other in everyone:
        pl.semaphore_signal(barrier, inc=1, device_id=other, device_id_type=MESH)

    copies = [
        pltpu.make_async_copy(a, b, local_sems.at[i])
        for i, (a, b) in enumerate(
            (
                (features, held.at[rep]),
                (dst_hbm, dst_ref),
                (src_hbm, src_ref),
                (tiles_hbm, tiles),
                (weights_hbm, weights),
                (biases_hbm, biases),
            )
        )
    ]
    for copy in copies:
        copy.start()
    own_in, dst_in, src_in, tiles_in, *later_in = copies
    table_in = pltpu.make_async_copy(table_v, table, local_sems.at[len(copies)])

    def tables():
        merged[SLOTS] = jnp.zeros((B, B), jnp.bfloat16)
        dst_in.wait()
        src_in.wait()
        table_v[...] = jnp.zeros_like(table_v)
        for i, row in enumerate(order_tables(dst_ref[...], src_ref[...], count_ref[0])):
            table_v[pl.ds(i, 1), :] = row
        table_in.start()
        tiles_in.wait()
        table_in.wait()

    def merge():
        def step(i, run):
            for q in range(4):
                q = 4 * i + q
                run = jnp.where(table[5, q] > 0, run, 0.0) + tiles[table[4, q]].astype(jnp.float32)
                merged[q] = run.astype(jnp.bfloat16)
            return run

        lax.fori_loop(0, SLOTS // 4, step, jnp.zeros((B, B), jnp.float32))

    def partial_copy(k, d):
        return pltpu.make_async_remote_copy(
            src_ref=outbox.at[k * NL + d],
            dst_ref=inbox.at[k * NL + d],
            send_sem=sent_sems.at[LAYERS + k],
            recv_sem=recv_sems.at[k * NSEM + RS + d],
            device_id=mates[d - 1],
            device_id_type=MESH,
        )

    def layer(k, unused):
        def link(ref, sem, device):
            return pltpu.make_async_remote_copy(
                src_ref=ref,
                dst_ref=ref,
                send_sem=sent_sems.at[k],
                recv_sem=recv_sems.at[k * NSEM + sem],
                device_id=device,
                device_id_type=MESH,
            )

        def send(ref, sem, device):
            link(ref, sem, device).start()

        def landed(ref, sem):
            link(ref, sem, y_up).wait_recv()

        def block(off, dy):
            return k * NREP + zmod(z + off) * NY + ymod(y + dy)

        def rows_a(off, dy):
            return held.at[block(off, dy), pl.ds(0, RA), :]

        def rows_b(off, dy=0, part=None):
            if part is None:
                return held.at[block(off, dy), pl.ds(RA, RB), :]
            return held.at[block(off, dy), pl.ds(RA, CUT) if part else pl.ds(RA + CUT, RB - CUT), :]

        def towards(up, i):
            return (1 if up else -1) * (face if i < HALF - 1 else 1)

        def turned(off):
            off = off if off <= HALF else off - NZ
            return off * face if abs(off) < HALF - 1 else off

        def piece(what, leaving):
            kind, *which = what
            if kind == "zb":
                up, i, part = which
                way = towards(up, i)
                ref = rows_b(-way * (i - leaving), 0, None if part == 2 else part == 0)
                return ref, ZB + (2 * (part % 2) + (1 - way) // 2) * (HALF + 1) + i, at(zmod(z + way), y)
            if kind == "za":
                dy, up, i = which
                way = towards(up, i)
                sem = ZA + (2 * dy + (1 - way) // 2) * (HALF + 1) + i
                return rows_a(-way * (i - leaving), dy), sem, at(zmod(z + way), y)
            if kind == "ya":
                dy = which[0]
                return rows_a(0, 0 if leaving else -dy), YA + dy, (None, y_up, y_far, y_down)[dy]
            hop, place, _ = which
            off = turned(place)
            up = hop == 0 or (hop == 2 and place % 2 == 0)
            sem = YB + hop * NZ + zmod(off)
            if hop == 2:
                return rows_b(off, (-1 if up else 1) if leaving else 2), sem, y_up if up else y_down
            return rows_b(off, 0 if leaving else (-1 if up else 1)), sem, y_up if up else y_down

        def group(off):
            zz = zmod(z + off) * NY
            right = held[pl.ds(k * NREP + zz, NY)].reshape(NY * B, F)

            def product(d):
                cell = lax.rem(me + d, NL) * NREP + zz
                line, at0 = cell // B, lax.rem(cell, B)
                left = jnp.concatenate([merged[table[line, at0 + yy]] for yy in range(NY)], axis=1)
                return jnp.dot(left, right, preferred_element_type=jnp.float32)

            return product

        def take(step):
            ref, sem, device = piece(step[1:], step[0] == "s")
            if step[0] == "s":
                send(ref, sem, device)
            else:
                landed(ref, sem)

        opening = min(n for n, step in enumerate(ORDER) if step[0] == "w")
        for step in ORDER[:opening]:
            take(step)

        @pl.when(k == 0)
        def _():
            tables()
            merge()
            for copy in later_in:
                copy.wait()

        begun = False
        late = []
        final = max(n for n, step in enumerate(ORDER) if step[0] == "w")
        for n, step in enumerate(ORDER[opening:], opening):
            if step[0] != "g":
                take(step)
            elif n > final:
                late.append(turned(step[1]))
            else:
                product = group(turned(step[1]))
                for d in range(NL):
                    part = product(d)
                    total[d] = total[d] + part if begun else part
                begun = True
        late = [group(off) for off in late]
        for d in (4, 3, 5, 2, 6, 1, 7, 0):
            part = total[d]
            for product in late:
                part = part + product(d)
            if d:
                outbox[k * NL + d] = part.astype(jnp.bfloat16)
                partial_copy(k, d).start()
        for d in (1, 7, 2, 6, 3, 5, 4):
            partial_copy(k, d).wait_recv()
            part = part + inbox[k * NL + d].astype(jnp.float32)
        mixed = jnp.dot(part.astype(jnp.bfloat16), weights[k], preferred_element_type=jnp.float32)
        hidden = jnp.maximum(mixed + biases[pl.ds(k, 1), :], 0.0).astype(jnp.bfloat16)

        @pl.when(k + 1 < LAYERS)
        def _():
            held[(k + 1) * NREP + rep] = hidden

        @pl.when(k + 1 == LAYERS)
        def _():
            out[...] = hidden

        return unused

    own_in.wait()
    pl.semaphore_wait(barrier, len(everyone))
    lax.fori_loop(0, LAYERS, layer, 0)
    for k in range(LAYERS):
        for buffer, sem, blocks in ((held, k, NREP - 1), (outbox, LAYERS + k, NL - 1)):
            whole = buffer.at[pl.ds(0, blocks)]
            pltpu.make_async_remote_copy(
                src_ref=whole,
                dst_ref=whole,
                send_sem=sent_sems.at[sem],
                recv_sem=recv_sems.at[0],
                device_id=y_up,
                device_id_type=MESH,
            ).wait_send()


def body(features, tiles, tile_dst, tile_src, tile_count, weights, biases):
    vmem, anyspace = pl.BlockSpec(memory_space=pltpu.VMEM), pl.BlockSpec(memory_space=pl.ANY)
    smem = pl.BlockSpec(memory_space=pltpu.SMEM)
    return pl.pallas_call(
        kernel,
        out_shape=jax.ShapeDtypeStruct((B, F), jnp.bfloat16),
        in_specs=[anyspace, anyspace, anyspace, anyspace, smem, anyspace, anyspace],
        out_specs=vmem,
        scratch_shapes=[
            pltpu.VMEM((LAYERS * NREP, B, F), jnp.bfloat16),
            pltpu.VMEM((SLOTS, B, B), jnp.bfloat16),
            pltpu.VMEM((SLOTS + 1, B, B), jnp.bfloat16),
            pltpu.VMEM((1, SLOTS), jnp.int32),
            pltpu.VMEM((1, SLOTS), jnp.int32),
            pltpu.VMEM((LAYERS, F, F), jnp.bfloat16),
            pltpu.VMEM((LAYERS, F), jnp.float32),
            pltpu.VMEM((8, B), jnp.int32),
            pltpu.SMEM((8, B), jnp.int32),
            pltpu.VMEM((NL, B, F), jnp.float32),
            pltpu.VMEM((LAYERS * NL, B, F), jnp.bfloat16),
            pltpu.VMEM((LAYERS * NL, B, F), jnp.bfloat16),
            pltpu.SemaphoreType.DMA((2 * LAYERS,)),
            pltpu.SemaphoreType.DMA((LAYERS * NSEM,)),
            pltpu.SemaphoreType.DMA((8,)),
        ],
        compiler_params=pltpu.CompilerParams(
            collective_id=0, has_side_effects=True, vmem_limit_bytes=VMEM
        ),
        cost_estimate=pl.CostEstimate(flops=2 * LAYERS * CELLS * B * B * F, bytes_accessed=4 << 20, transcendentals=0),
    )(
        features,
        tiles,
        tile_dst.reshape(1, SLOTS),
        tile_src.reshape(1, SLOTS),
        tile_count,
        weights,
        biases,
    )


def solution(mesh):
    in_specs = (
        P(("rep", "loop"), None),
        P(("rep", "loop"), None, None),
        P(("rep", "loop")),
        P(("rep", "loop")),
        P(("rep", "loop")),
        P(),
        P(),
    )
    out_specs = P(("rep", "loop"), None)
    return jax.shard_map(body, mesh=mesh, in_specs=in_specs, out_specs=out_specs, check_vma=False)
```

```python
import jax
import jax.numpy as jnp
from jax import lax
from jax.experimental import pallas as pl
from jax.experimental.pallas import tpu as pltpu
from jax.sharding import PartitionSpec as P

MESH = pl.DeviceIdType.MESH
NZ, NY, NL = 16, 4, 8
NREP = NZ * NY
B = 128
F = 256
SLOTS = 96
LAYERS = 2
RA = 48
RB = B - RA
CUT = 48
VMEM = 62 * 1024 * 1024
HALF = NZ // 2
CELLS = NL * NREP
ZB, ZA = 0, 4 * (HALF + 1)
YA = ZA + NY * 2 * (HALF + 1)
YB = YA + NY
RS = YB + 3 * NZ
NSEM = RS + NL
ORDER = (
    ("s", "zb", 0, 1, 0), ("s", "ya", 1), ("s", "ya", 3), ("s", "zb", 1, 1, 0), ("s", "zb", 1, 1, 1), ("s", "ya", 2),
    ("s", "zb", 0, 1, 1), ("s", "za", 0, 1, 1), ("s", "za", 0, 0, 1), ("w", "zb", 0, 1, 0), ("s", "zb", 0, 2, 0),
    ("w", "zb", 0, 1, 1), ("s", "zb", 0, 2, 1), ("w", "zb", 1, 1, 0), ("s", "zb", 1, 2, 0), ("w", "ya", 1),
    ("s", "za", 3, 0, 1), ("w", "zb", 1, 1, 1), ("w", "za", 0, 0, 1), ("s", "yb", 1, 1, 2), ("s", "za", 0, 0, 2),
    ("s", "zb", 1, 2, 1), ("s", "za", 3, 1, 1), ("w", "ya", 3), ("s", "za", 1, 0, 1), ("s", "yb", 1, 15, 2),
    ("s", "yb", 0, 15, 2), ("w", "za", 0, 1, 1), ("s", "za", 0, 1, 2), ("s", "za", 1, 1, 1), ("w", "zb", 0, 2, 0),
    ("s", "zb", 0, 3, 0), ("w", "zb", 1, 2, 0), ("s", "yb", 0, 0, 2), ("s", "zb", 1, 3, 0), ("w", "zb", 0, 2, 1),
    ("s", "zb", 0, 3, 1), ("w", "za", 3, 0, 1), ("w", "zb", 1, 2, 1), ("s", "za", 3, 0, 2), ("s", "zb", 1, 3, 1),
    ("w", "za", 3, 1, 1), ("s", "za", 3, 1, 2), ("w", "ya", 2), ("s", "za", 2, 0, 1), ("s", "yb", 1, 0, 2),
    ("s", "za", 2, 1, 1), ("s", "yb", 1, 14, 2), ("s", "yb", 1, 2, 2), ("s", "yb", 0, 14, 2), ("w", "za", 0, 1, 2),
    ("w", "za", 1, 1, 1), ("w", "za", 1, 0, 1), ("s", "za", 1, 0, 2), ("w", "za", 0, 0, 2), ("s", "za", 1, 1, 2),
    ("w", "yb", 1, 1, 2), ("s", "za", 0, 0, 3), ("w", "zb", 0, 3, 0), ("s", "yb", 0, 1, 2), ("s", "yb", 0, 2, 2),
    ("s", "zb", 0, 4, 0), ("s", "za", 0, 1, 3), ("w", "zb", 1, 3, 0), ("s", "zb", 1, 4, 0), ("w", "zb", 0, 3, 1),
    ("s", "zb", 0, 4, 1), ("w", "yb", 1, 15, 2), ("s", "yb", 2, 15, 2), ("w", "zb", 1, 3, 1), ("w", "yb", 0, 0, 2),
    ("s", "zb", 1, 4, 1), ("s", "yb", 0, 13, 2), ("w", "za", 2, 0, 1), ("s", "za", 2, 0, 2), ("w", "za", 3, 1, 2),
    ("w", "za", 3, 0, 2), ("s", "za", 3, 1, 3), ("w", "za", 2, 1, 1), ("s", "yb", 1, 3, 2), ("s", "za", 3, 0, 3),
    ("s", "yb", 1, 13, 2), ("s", "za", 2, 1, 2), ("w", "za", 1, 0, 2), ("s", "za", 1, 0, 3), ("w", "yb", 1, 0, 2),
    ("w", "za", 1, 1, 2), ("s", "za", 1, 1, 3), ("s", "yb", 0, 3, 2), ("w", "za", 0, 1, 3), ("w", "za", 0, 0, 3),
    ("w", "zb", 0, 4, 0), ("s", "zb", 0, 5, 0), ("w", "zb", 1, 4, 0), ("s", "zb", 1, 5, 0), ("w", "zb", 0, 4, 1),
    ("s", "zb", 0, 5, 1), ("w", "zb", 1, 4, 1), ("s", "zb", 1, 5, 1), ("s", "za", 0, 1, 4), ("s", "za", 0, 0, 4),
    ("s", "yb", 0, 12, 2), ("w", "za", 2, 0, 2), ("s", "za", 2, 0, 3), ("w", "za", 2, 1, 2), ("s", "za", 2, 1, 3),
    ("w", "yb", 0, 2, 2), ("s", "yb", 1, 12, 2), ("s", "yb", 0, 4, 2), ("w", "yb", 2, 15, 2), ("w", "za", 3, 0, 3),
    ("w", "za", 3, 1, 3), ("s", "za", 3, 0, 4), ("s", "za", 3, 1, 4), ("w", "za", 1, 0, 3), ("s", "yb", 2, 1, 2),
    ("w", "yb", 1, 3, 2), ("w", "za", 1, 1, 3), ("s", "za", 1, 0, 4), ("w", "yb", 1, 2, 2), ("s", "yb", 2, 3, 2),
    ("s", "za", 1, 1, 4), ("w", "zb", 0, 5, 0), ("w", "yb", 0, 14, 2), ("s", "zb", 0, 6, 0), ("s", "yb", 2, 0, 2),
    ("w", "zb", 1, 5, 0), ("s", "zb", 1, 6, 0), ("w", "zb", 0, 5, 1), ("s", "yb", 2, 2, 2), ("s", "zb", 0, 6, 1),
    ("w", "zb", 1, 5, 1), ("w", "za", 0, 0, 4), ("s", "zb", 1, 6, 1), ("w", "za", 0, 1, 4), ("s", "za", 0, 0, 5),
    ("s", "yb", 1, 5, 2), ("s", "za", 0, 1, 5), ("s", "yb", 0, 5, 2), ("w", "za", 2, 0, 3), ("s", "za", 2, 0, 4),
    ("s", "yb", 1, 11, 2), ("w", "za", 2, 1, 3), ("s", "za", 2, 1, 4), ("w", "za", 3, 1, 4), ("w", "za", 3, 0, 4),
    ("s", "yb", 2, 14, 2), ("w", "za", 1, 0, 4), ("s", "za", 1, 0, 5), ("s", "za", 3, 1, 5), ("s", "za", 3, 0, 5),
    ("w", "za", 1, 1, 4), ("s", "za", 1, 1, 5), ("s", "yb", 1, 4, 2), ("w", "zb", 0, 6, 0), ("w", "zb", 1, 6, 0),
    ("w", "yb", 0, 4, 2), ("s", "zb", 1, 7, 0), ("w", "yb", 0, 3, 2), ("w", "zb", 0, 6, 1), ("s", "yb", 0, 6, 2),
    ("w", "zb", 1, 6, 1), ("s", "zb", 0, 7, 1), ("s", "yb", 1, 6, 2), ("w", "yb", 0, 15, 2), ("w", "yb", 0, 12, 2),
    ("s", "yb", 0, 10, 2), ("s", "zb", 1, 7, 1), ("s", "zb", 0, 7, 0), ("w", "yb", 2, 2, 2), ("w", "yb", 2, 3, 2),
    ("w", "za", 2, 0, 4), ("s", "za", 2, 0, 5), ("w", "za", 0, 0, 5), ("w", "yb", 1, 14, 2), ("w", "za", 2, 1, 4),
    ("s", "za", 2, 1, 5), ("s", "za", 0, 0, 6), ("w", "za", 0, 1, 5), ("w", "yb", 1, 5, 2), ("s", "yb", 2, 12, 2),
    ("s", "yb", 2, 4, 2), ("s", "yb", 1, 10, 2), ("g", 15), ("w", "yb", 2, 1, 2), ("w", "za", 1, 0, 5),
    ("s", "za", 1, 0, 6), ("s", "za", 0, 1, 6), ("s", "yb", 0, 11, 2), ("s", "yb", 2, 5, 2), ("w", "za", 3, 0, 5),
    ("s", "za", 3, 0, 6), ("w", "yb", 1, 13, 2), ("w", "za", 1, 1, 5), ("s", "za", 1, 1, 6), ("g", 2),
    ("w", "yb", 2, 0, 2), ("w", "yb", 0, 5, 2), ("w", "za", 3, 1, 5), ("s", "za", 3, 1, 6), ("s", "yb", 2, 13, 2),
    ("w", "zb", 1, 7, 0), ("s", "zb", 1, 8, 0), ("w", "zb", 0, 7, 1), ("s", "zb", 0, 8, 1), ("g", 3),
    ("w", "zb", 1, 7, 1), ("s", "yb", 1, 9, 2), ("w", "yb", 1, 6, 2), ("w", "zb", 0, 7, 0), ("w", "yb", 0, 6, 2),
    ("s", "yb", 2, 6, 2), ("w", "za", 2, 1, 5), ("s", "za", 2, 1, 6), ("w", "za", 2, 0, 5), ("s", "za", 2, 0, 6),
    ("w", "yb", 2, 14, 2), ("s", "yb", 1, 7, 2), ("g", 0), ("w", "za", 0, 0, 6), ("s", "yb", 0, 9, 2),
    ("w", "za", 0, 1, 6), ("s", "za", 0, 1, 7), ("w", "yb", 0, 10, 2), ("s", "za", 0, 0, 7), ("g", 14),
    ("w", "yb", 1, 11, 2), ("w", "za", 1, 0, 6), ("w", "za", 1, 1, 6), ("s", "za", 1, 1, 7), ("w", "yb", 1, 12, 2),
    ("s", "yb", 2, 11, 2), ("w", "za", 3, 0, 6), ("w", "yb", 2, 4, 2), ("w", "za", 3, 1, 6), ("s", "za", 3, 0, 7),
    ("w", "yb", 2, 12, 2), ("w", "zb", 0, 8, 1), ("w", "zb", 1, 8, 0), ("s", "yb", 0, 8, 2), ("s", "yb", 1, 8, 2),
    ("w", "yb", 1, 4, 2), ("s", "za", 3, 1, 7), ("w", "za", 2, 0, 6), ("w", "yb", 2, 5, 2), ("g", 5),
    ("s", "yb", 2, 10, 2), ("w", "yb", 2, 13, 2), ("g", 12), ("w", "yb", 0, 13, 2), ("w", "yb", 1, 9, 2),
    ("w", "yb", 0, 11, 2), ("s", "za", 1, 0, 7), ("s", "yb", 2, 9, 2), ("w", "za", 2, 1, 6), ("s", "za", 2, 0, 7),
    ("w", "yb", 2, 6, 2), ("s", "za", 2, 1, 7), ("s", "yb", 0, 7, 2), ("g", 13), ("w", "za", 0, 1, 7),
    ("w", "yb", 1, 7, 2), ("s", "za", 0, 1, 8), ("s", "yb", 2, 7, 2), ("g", 4), ("w", "za", 1, 1, 7),
    ("s", "za", 1, 1, 8), ("w", "za", 3, 0, 7), ("s", "za", 3, 0, 8), ("w", "yb", 0, 1, 2), ("w", "yb", 1, 10, 2),
    ("w", "yb", 0, 8, 2), ("s", "yb", 2, 8, 2), ("w", "za", 2, 0, 7), ("s", "za", 2, 0, 8), ("w", "yb", 0, 9, 2),
    ("g", 1), ("w", "yb", 1, 8, 2), ("w", "yb", 2, 11, 2), ("g", 11), ("g", 6), ("w", "yb", 2, 10, 2),
    ("w", "za", 0, 0, 7), ("g", 10), ("w", "yb", 2, 9, 2), ("w", "za", 3, 1, 7), ("w", "za", 2, 1, 7),
    ("w", "za", 1, 0, 7), ("g", 9), ("w", "yb", 0, 7, 2), ("w", "yb", 2, 7, 2), ("g", 7), ("w", "za", 0, 1, 8),
    ("w", "za", 1, 1, 8), ("w", "za", 3, 0, 8), ("w", "yb", 2, 8, 2), ("w", "za", 2, 0, 8), ("g", 8),
)


def order_tables(dst, src, count):
    n = SLOTS
    i32 = jnp.int32
    row = lax.broadcasted_iota(i32, (n, n), 0)
    col = lax.broadcasted_iota(i32, (n, n), 1)
    lane = lax.broadcasted_iota(i32, (1, n), 1)
    key_row = jnp.where(lane < count, dst * NREP + src, CELLS)
    key = jnp.sum(jnp.where(row == col, key_row, 0), axis=1, keepdims=True)
    before = (key_row < key) | ((key_row == key) & (col < row))
    place = jnp.sum(jnp.where(before, 1, 0), axis=1, keepdims=True)
    lanes = lax.broadcasted_iota(i32, (n, B), 1)
    slot = lax.broadcasted_iota(i32, (n, B), 0)
    rows = []
    for part in range(CELLS // B):
        last = jnp.max(jnp.where(key == lanes + part * B, place, -1), axis=0, keepdims=True)
        rows.append(jnp.where(last < 0, SLOTS, last))
    here = place == lanes
    rows.append(jnp.sum(jnp.where(here, slot, 0), axis=0, keepdims=True))
    mine = jnp.sum(jnp.where(here, key, 0), axis=0, keepdims=True)
    prior = jnp.sum(jnp.where(place + 1 == lanes, key, 0), axis=0, keepdims=True)
    rows.append(jnp.where((mine == prior) & (lanes[:1] > 0), 1, 0))
    return rows


def kernel(
    features,
    tiles_hbm,
    dst_hbm,
    src_hbm,
    count_ref,
    weights_hbm,
    biases_hbm,
    out,
    held,
    tiles,
    merged,
    dst_ref,
    src_ref,
    weights,
    biases,
    table_v,
    table,
    total,
    outbox,
    inbox,
    sent_sems,
    recv_sems,
    local_sems,
):
    rep = lax.axis_index("rep")
    me = lax.axis_index("loop")
    z = rep // NY
    y = rep % NY
    face = 1 - 2 * (lax.rem(z, 4) // 2)

    def zmod(v):
        return lax.rem(v + 2 * NZ, NZ)

    def ymod(v):
        return lax.rem(v + 2 * NY, NY)

    def at(zz, yy):
        return {"rep": zz * NY + yy}

    y_up, y_down, y_far = at(z, ymod(y + 1)), at(z, ymod(y - 1)), at(z, ymod(y + 2))
    mates = [{"loop": lax.rem(me + d, NL)} for d in range(1, NL)]

    barrier = pltpu.get_barrier_semaphore()
    everyone = [at(zmod(z + 1), y), at(zmod(z - 1), y), y_up, y_down, y_far] + mates
    for other in everyone:
        pl.semaphore_signal(barrier, inc=1, device_id=other, device_id_type=MESH)

    copies = [
        pltpu.make_async_copy(a, b, local_sems.at[i])
        for i, (a, b) in enumerate(
            (
                (features, held.at[rep]),
                (dst_hbm, dst_ref),
                (src_hbm, src_ref),
                (tiles_hbm, tiles),
                (weights_hbm, weights),
                (biases_hbm, biases),
            )
        )
    ]
    for copy in copies:
        copy.start()
    own_in, dst_in, src_in, tiles_in, *later_in = copies
    table_in = pltpu.make_async_copy(table_v, table, local_sems.at[len(copies)])

    def tables():
        merged[SLOTS] = jnp.zeros((B, B), jnp.bfloat16)
        dst_in.wait()
        src_in.wait()
        table_v[...] = jnp.zeros_like(table_v)
        for i, row in enumerate(order_tables(dst_ref[...], src_ref[...], count_ref[0])):
            table_v[pl.ds(i, 1), :] = row
        table_in.start()
        tiles_in.wait()
        table_in.wait()

    def merge():
        def step(i, run):
            for q in range(4):
                q = 4 * i + q
                run = jnp.where(table[5, q] > 0, run, 0.0) + tiles[table[4, q]].astype(jnp.float32)
                merged[q] = run.astype(jnp.bfloat16)
            return run

        lax.fori_loop(0, SLOTS // 4, step, jnp.zeros((B, B), jnp.float32))

    def partial_copy(k, d):
        return pltpu.make_async_remote_copy(
            src_ref=outbox.at[k * NL + d],
            dst_ref=inbox.at[k * NL + d],
            send_sem=sent_sems.at[LAYERS + k],
            recv_sem=recv_sems.at[k * NSEM + RS + d],
            device_id=mates[d - 1],
            device_id_type=MESH,
        )

    def layer(k, unused):
        def link(ref, sem, device):
            return pltpu.make_async_remote_copy(
                src_ref=ref,
                dst_ref=ref,
                send_sem=sent_sems.at[k],
                recv_sem=recv_sems.at[k * NSEM + sem],
                device_id=device,
                device_id_type=MESH,
            )

        def send(ref, sem, device):
            link(ref, sem, device).start()

        def landed(ref, sem):
            link(ref, sem, y_up).wait_recv()

        def block(off, dy):
            return k * NREP + zmod(z + off) * NY + ymod(y + dy)

        def rows_a(off, dy):
            return held.at[block(off, dy), pl.ds(0, RA), :]

        def rows_b(off, dy=0, part=None):
            if part is None:
                return held.at[block(off, dy), pl.ds(RA, RB), :]
            return held.at[block(off, dy), pl.ds(RA, CUT) if part else pl.ds(RA + CUT, RB - CUT), :]

        def towards(up, i):
            return (1 if up else -1) * (face if i < HALF - 1 else 1)

        def turned(off):
            off = off if off <= HALF else off - NZ
            return off * face if abs(off) < HALF - 1 else off

        def piece(what, leaving):
            kind, *which = what
            if kind == "zb":
                up, i, part = which
                way = towards(up, i)
                ref = rows_b(-way * (i - leaving), 0, None if part == 2 else part == 0)
                return ref, ZB + (2 * (part % 2) + (1 - way) // 2) * (HALF + 1) + i, at(zmod(z + way), y)
            if kind == "za":
                dy, up, i = which
                way = towards(up, i)
                sem = ZA + (2 * dy + (1 - way) // 2) * (HALF + 1) + i
                return rows_a(-way * (i - leaving), dy), sem, at(zmod(z + way), y)
            if kind == "ya":
                dy = which[0]
                return rows_a(0, 0 if leaving else -dy), YA + dy, (None, y_up, y_far, y_down)[dy]
            hop, place, _ = which
            off = turned(place)
            up = hop == 0 or (hop == 2 and place % 2 == 0)
            sem = YB + hop * NZ + zmod(off)
            if hop == 2:
                return rows_b(off, (-1 if up else 1) if leaving else 2), sem, y_up if up else y_down
            return rows_b(off, 0 if leaving else (-1 if up else 1)), sem, y_up if up else y_down

        def group(off):
            zz = zmod(z + off) * NY
            right = held[pl.ds(k * NREP + zz, NY)].reshape(NY * B, F)

            def product(d):
                cell = lax.rem(me + d, NL) * NREP + zz
                line, at0 = cell // B, lax.rem(cell, B)
                left = jnp.concatenate([merged[table[line, at0 + yy]] for yy in range(NY)], axis=1)
                return jnp.dot(left, right, preferred_element_type=jnp.float32)

            return product

        def take(step):
            ref, sem, device = piece(step[1:], step[0] == "s")
            if step[0] == "s":
                send(ref, sem, device)
            else:
                landed(ref, sem)

        opening = min(n for n, step in enumerate(ORDER) if step[0] == "w")
        for step in ORDER[:opening]:
            take(step)

        @pl.when(k == 0)
        def _():
            tables()
            merge()
            for copy in later_in:
                copy.wait()

        begun = False
        late = []
        final = max(n for n, step in enumerate(ORDER) if step[0] == "w")
        for n, step in enumerate(ORDER[opening:], opening):
            if step[0] != "g":
                take(step)
            elif n > final:
                late.append(turned(step[1]))
            else:
                product = group(turned(step[1]))
                for d in range(NL):
                    part = product(d)
                    total[d] = total[d] + part if begun else part
                begun = True
        late = [group(off) for off in late]
        for d in (4, 3, 5, 2, 6, 1, 7, 0):
            part = total[d]
            for product in late:
                part = part + product(d)
            if d:
                outbox[k * NL + d] = part.astype(jnp.bfloat16)
                partial_copy(k, d).start()
        for d in (1, 7, 2, 6, 3, 5, 4):
            partial_copy(k, d).wait_recv()
            part = part + inbox[k * NL + d].astype(jnp.float32)
        mixed = jnp.dot(part.astype(jnp.bfloat16), weights[k], preferred_element_type=jnp.float32)
        hidden = jnp.maximum(mixed + biases[pl.ds(k, 1), :], 0.0).astype(jnp.bfloat16)

        @pl.when(k + 1 < LAYERS)
        def _():
            held[(k + 1) * NREP + rep] = hidden

        @pl.when(k + 1 == LAYERS)
        def _():
            out[...] = hidden

        return unused

    own_in.wait()
    pl.semaphore_wait(barrier, len(everyone))
    lax.fori_loop(0, LAYERS, layer, 0)
    for k in range(LAYERS):
        for buffer, sem, blocks in ((held, k, NREP - 1), (outbox, LAYERS + k, NL - 1)):
            whole = buffer.at[pl.ds(0, blocks)]
            pltpu.make_async_remote_copy(
                src_ref=whole,
                dst_ref=whole,
                send_sem=sent_sems.at[sem],
                recv_sem=recv_sems.at[0],
                device_id=y_up,
                device_id_type=MESH,
            ).wait_send()


def body(features, tiles, tile_dst, tile_src, tile_count, weights, biases):
    vmem, anyspace = pl.BlockSpec(memory_space=pltpu.VMEM), pl.BlockSpec(memory_space=pl.ANY)
    smem = pl.BlockSpec(memory_space=pltpu.SMEM)
    return pl.pallas_call(
        kernel,
        out_shape=jax.ShapeDtypeStruct((B, F), jnp.bfloat16),
        in_specs=[anyspace, anyspace, anyspace, anyspace, smem, anyspace, anyspace],
        out_specs=vmem,
        scratch_shapes=[
            pltpu.VMEM((LAYERS * NREP, B, F), jnp.bfloat16),
            pltpu.VMEM((SLOTS, B, B), jnp.bfloat16),
            pltpu.VMEM((SLOTS + 1, B, B), jnp.bfloat16),
            pltpu.VMEM((1, SLOTS), jnp.int32),
            pltpu.VMEM((1, SLOTS), jnp.int32),
            pltpu.VMEM((LAYERS, F, F), jnp.bfloat16),
            pltpu.VMEM((LAYERS, F), jnp.float32),
            pltpu.VMEM((8, B), jnp.int32),
            pltpu.SMEM((8, B), jnp.int32),
            pltpu.VMEM((NL, B, F), jnp.float32),
            pltpu.VMEM((LAYERS * NL, B, F), jnp.bfloat16),
            pltpu.VMEM((LAYERS * NL, B, F), jnp.bfloat16),
            pltpu.SemaphoreType.DMA((2 * LAYERS,)),
            pltpu.SemaphoreType.DMA((LAYERS * NSEM,)),
            pltpu.SemaphoreType.DMA((8,)),
        ],
        compiler_params=pltpu.CompilerParams(
            collective_id=0, has_side_effects=True, vmem_limit_bytes=VMEM
        ),
        cost_estimate=pl.CostEstimate(flops=2 * LAYERS * CELLS * B * B * F, bytes_accessed=4 << 20, transcendentals=0),
    )(
        features,
        tiles,
        tile_dst.reshape(1, SLOTS),
        tile_src.reshape(1, SLOTS),
        tile_count,
        weights,
        biases,
    )


def solution(mesh):
    in_specs = (
        P(("rep", "loop"), None),
        P(("rep", "loop"), None, None),
        P(("rep", "loop")),
        P(("rep", "loop")),
        P(("rep", "loop")),
        P(),
        P(),
    )
    out_specs = P(("rep", "loop"), None)
    return jax.shard_map(body, mesh=mesh, in_specs=in_specs, out_specs=out_specs, check_vma=False)
```
